256 devices in a mesh: outer: 16 (over y, z_hi), inner: 16 (over x, z_lo, core).
Axes of the slice: x: 4, y: 4, z: 8 (z_hi: 4, z_lo: 2; z = z_hi * 2 + z_lo), core: 2. Of those that a mesh axis runs over, the one named last changes fastest.
Arguments:
- hidden: bfloat16 [32768, 1024], P(('outer', 'inner')), may hold values from -24 to 24
- x_act: bfloat16 [32768, 2048], P(('outer', 'inner')), may hold values from -6 to 6
- dt_step: float32 [32768, 32], P(('outer', 'inner')), may hold values from 0.0014915534 to 0.44, as said below
- log_decay: float32 [32768, 32], P(('outer', 'inner')), may hold values from -0.81 to -8.85009766e-07, as said below
- w_bc: bfloat16 [1024, 128], P(('outer', 'inner')), may hold values from -0.1875 to 0.1875
- grad_y: bfloat16 [32768, 2048], P(('outer', 'inner')), may hold values from -0.19921875 to 0.19921875
Outputs:
- grad_x: float32 [32768, 2048], P(('outer', 'inner'))
- grad_hidden: float32 [32768, 1024], P(('outer', 'inner'))
- grad_proj: float32 [1024, 128], P(('outer', 'inner'))
The draws below stay inside these ranges and needn't reach their ends.
Inputs may be any that keep to these rules, and one draw needn't show every extreme that they name: `dt_step`: Positive; constant in scale within each head apart from a factor within e**-0.5 to e**0.5. `log_decay`: Negative.
All inputs are finite; a program needn't handle non-finite values.
Results may differ from the reference program's by a relative error of at most 0.0029.
Values may be sent and summed in bfloat16 or wider, within the bound.
A program may use at most 64 MiB of HBM per device.

```python
import math
import jax
import jax.numpy as jnp
from jax import lax

D = 1024
HEADS = 32
HEAD = 64
STATE = 64
BLOCK = 128
TOK_DEV = 128
TOKENS = 32768


def head_rates(key):
    pick_key = jax.random.fold_in(key, 11)
    slow_key = jax.random.fold_in(key, 12)
    fast_key = jax.random.fold_in(key, 13)
    slow_share = 5
    picks = jax.random.randint(pick_key, (HEADS,), 0, 8)
    slow_rate = jnp.exp(jax.random.uniform(slow_key, (HEADS,), jnp.float32, math.log(0.1), math.log(0.35))) / TOKENS
    fast_rate = jnp.exp(jax.random.uniform(fast_key, (HEADS,), jnp.float32, math.log(0.02), math.log(0.035)))
    return jnp.where(picks < slow_share, slow_rate, fast_rate)


def draw_dt_step(key, part):
    forgetting_speeds = head_rates(key)
    approximate_guess = jax.random.uniform(jax.random.fold_in(key, 21), (TOKENS, HEADS), jnp.float32, -0.5, 0.5)
    return jnp.sqrt(2.0 * forgetting_speeds)[None, :] * jnp.exp(approximate_guess)


def draw_log_decay(key, part):
    forgetting_speeds = head_rates(key)
    blocks = TOKENS // TOK_DEV
    multiplier_coefficient = jnp.exp(jax.random.uniform(jax.random.fold_in(key, 31), (blocks, HEADS), jnp.float32, math.log(0.6), math.log(1.6)))
    multiplier_coefficient = jnp.repeat(multiplier_coefficient, TOK_DEV, axis=0)
    approximate_guess = jnp.exp(jax.random.uniform(jax.random.fold_in(key, 32), (TOKENS, HEADS), jnp.float32, -0.7, 0.7))
    accelerator_slots = jax.random.randint(jax.random.fold_in(key, 33), (2,), 0, TOKENS)
    stack_height = jax.random.uniform(jax.random.fold_in(key, 34), (2, HEADS), jnp.float32, 0.22, 0.69)
    symbol_indices = jnp.arange(TOKENS)[:, None]
    run_span_count = jnp.where(symbol_indices == accelerator_slots[0], stack_height[0][None, :], 0.0) + jnp.where(symbol_indices == accelerator_slots[1], stack_height[1][None, :], 0.0)
    return -(forgetting_speeds[None, :] * multiplier_coefficient * approximate_guess) - run_span_count


def spiked(result, own_key, source, target, shards_of, factor):
    def block_of(position):
        return (jnp.arange(result.shape[position]) // (result.shape[position] // shards_of)).reshape((-1,) + (1,) * (result.ndim - 1 - position))

    near = jax.random.permutation(own_key, shards_of)[block_of(target)]
    far = (block_of(target) + shards_of // 2) % shards_of
    return jnp.where((block_of(source) == near) | (block_of(source) == far), factor * result, result)


def block_levels(own_key, shape, shards, low, high):
    def one(position, parts):
        heights = jax.random.uniform(jax.random.fold_in(jax.random.fold_in(own_key, 6), position), (parts,), jnp.float32, low / len(shards), high / len(shards))
        return jnp.repeat(jnp.exp(heights), shape[position] // parts).reshape((-1,) + (1,) * (len(shape) - position - 1))

    factor_of = one(*shards[0])
    for cut in shards[1:]:
        factor_of = factor_of * one(*cut)
    return factor_of


def scatter_about(key, shape, deviation, bound, cuts=(), dtype=jnp.bfloat16):
    entries = deviation * jax.random.normal(key, shape, jnp.float32)
    if cuts:
        entries = entries * block_levels(key, shape, cuts, -0.22, 0.18)
    return jnp.clip(entries, -bound, bound).astype(dtype)


def heavy_noise(stream_key, dims, scale, bound, split, heavy, kind=jnp.bfloat16):
    array = scale * jax.random.normal(stream_key, dims, jnp.float32)
    if split:
        array = array * block_levels(stream_key, dims, split, -0.22, 0.18)
    return jnp.clip(spiked(array, jax.random.fold_in(stream_key, 3), *heavy), -bound, bound).astype(kind)


def setup_inputs(seed: int = 0) -> dict:
    streams_of = jax.random.split(jax.random.key(seed), 7)
    return {
        "hidden": heavy_noise(streams_of[0], (TOKENS, D), 1.0, 24.0, ((0, 256),), (0, 1, 256, 6.0)),
        "x_act": scatter_about(streams_of[1], (TOKENS, HEADS * HEAD), 1.0, 6.0, ((0, 256),)),
        "dt_step": draw_dt_step(jax.random.fold_in(streams_of[6], 71), 0),
        "log_decay": draw_log_decay(jax.random.fold_in(streams_of[6], 71), 0),
        "w_bc": scatter_about(streams_of[4], (D, 2 * STATE), D ** -0.5, 0.1875, ((0, 256),)),
        "grad_y": scatter_about(streams_of[5], (TOKENS, HEADS * HEAD), 0.03125, 0.19921875, ((0, 256),)),
    }


HIGH = lax.Precision.HIGHEST

def block_step(carried, pieces):
    inputs, decays, b_rows, c_rows = pieces
    length = inputs.shape[0]
    running = jnp.cumsum(decays, axis=0)
    row_ids = lax.broadcasted_iota(jnp.int32, (length, length), 0)
    col_ids = lax.broadcasted_iota(jnp.int32, (length, length), 1)
    causal = row_ids >= col_ids
    spread = running.T[:, :, None] - running.T[:, None, :]
    segment = jnp.where(causal[None], jnp.exp(jnp.where(causal[None], spread, 0.0)), 0.0)
    scores = jnp.einsum('in,jn->ij', c_rows, b_rows, precision=HIGH)
    outputs = jnp.einsum('hij,jhp->ihp', segment * scores[None], inputs, precision=HIGH)
    outputs = outputs + jnp.exp(running)[:, :, None] * jnp.einsum('in,hpn->ihp', c_rows, carried, precision=HIGH)
    final_sum = running[-1]
    weights = jnp.exp(final_sum[None, :] - running)
    updated = jnp.exp(final_sum)[:, None, None] * carried + jnp.einsum('jhp,jn->hpn', inputs * weights[:, :, None], b_rows, precision=HIGH)
    return (updated, outputs)

def scan_block(inputs, decays, b_rows, c_rows, carried, length):
    count = inputs.shape[0] // length
    pieces = (inputs.reshape((count, length) + inputs.shape[1:]), decays.reshape((count, length, decays.shape[1])), b_rows.reshape((count, length, b_rows.shape[1])), c_rows.reshape((count, length, c_rows.shape[1])))
    final_state, outputs = lax.scan(jax.checkpoint(block_step), carried, pieces)
    return (outputs.reshape(inputs.shape), final_state)

def reference(hidden, x_act, dt_step, log_decay, w_bc, grad_y):
    projected = jnp.dot(hidden, w_bc, preferred_element_type=jnp.float32)
    b_rows = projected[:, :STATE]
    c_rows = projected[:, STATE:]
    inputs = dt_step[:, :, None] * x_act.astype(jnp.float32).reshape(TOKENS, HEADS, HEAD)
    cotangent = grad_y.astype(jnp.float32).reshape(TOKENS, HEADS, HEAD)
    start_state = jnp.zeros((HEADS, HEAD, STATE), jnp.float32)

    def forward(inputs, b_rows, c_rows):
        return scan_block(inputs, log_decay, b_rows, c_rows, start_state, BLOCK)[0]
    outputs, pullback = jax.vjp(forward, inputs, b_rows, c_rows)
    d_in, d_b, d_c = pullback(cotangent)
    grad_x = (dt_step[:, :, None] * d_in).reshape(TOKENS, HEADS * HEAD)
    d_proj = jnp.concatenate([d_b, d_c], axis=1)
    d_low = d_proj.astype(jnp.bfloat16)
    grad_hidden = lax.dot_general(d_low, w_bc, (((1,), (1,)), ((), ())), preferred_element_type=jnp.float32)
    grad_proj = lax.dot_general(hidden, d_low, (((0,), (0,)), ((), ())), preferred_element_type=jnp.float32) / math.sqrt(TOKENS)
    return (grad_x, grad_hidden, grad_proj)
```

```python
import functools
import math

import jax
import jax.numpy as jnp
from jax import lax
from jax.experimental import pallas as pl
from jax.experimental.pallas import tpu as pltpu
from jax.sharding import PartitionSpec as P

BF16 = jnp.bfloat16
F32 = jnp.float32
MESH = pl.DeviceIdType.MESH
HIGH = lax.Precision.HIGHEST

NN = (((1,), (0,)), ((), ()))
NT = (((1,), (1,)), ((), ()))

W_NEAR, W_FAR, S_OUT, S_FAR, S_BACK, S_HOME, G_FAR, G_NEAR = range(8)


def dot(a, b, dims=NN):
    return lax.dot_general(a, b, dims, preferred_element_type=F32)


def split(value):
    high = value.astype(BF16)
    return high, (value - high.astype(F32)).astype(BF16)


def dot3(a, b, dims=NN):
    a_high, a_low = split(a)
    b_high, b_low = split(b)
    return dot(a_high, b_high, dims) + dot(a_high, b_low, dims) + dot(a_low, b_high, dims)


def iota(shape, axis):
    return lax.broadcasted_iota(jnp.int32, shape, axis)


def kernel(
    scale, n_out, n_in,
    hidden_hbm, x_hbm, dt_ref, decay_ref, w_ref, gy_hbm,
    gx_hbm, gh_hbm, gp_ref,
    hidden, x, gy, hidden_t, gx, gh,
    w_near, w_far, grow, spread, xw_hi, xw_lo, gw_hi, gw_lo,
    s_send, s_recv, prefix, near_sum, o_send, o_recv, o_back, carry, s_back, s_home,
    g_send, g_recv, g_sum, g_near,
    load_sem, send_sem, recv_sem,
):
    me_out, me_in = lax.axis_index("outer"), lax.axis_index("inner")
    rows, width = hidden.shape
    lanes = x.shape[1]
    heads = dt_ref.shape[1]
    size = lanes // heads
    state = w_far.shape[2] // 2
    part = lanes // n_in
    far = 2 * state // n_out
    pairs = heads // 2

    loads = [
        pltpu.make_async_copy(source, target, load_sem.at[k])
        for k, (source, target) in enumerate(((x_hbm, x), (gy_hbm, gy), (hidden_hbm, hidden)))
    ]
    for load in loads:
        load.start()

    barrier = pltpu.get_barrier_semaphore()

    def each_near(act):
        lax.fori_loop(1, n_in, lambda k, c: (act(k, lax.rem(me_in + k, n_in)), c)[1], 0)

    def each_far(act):
        lax.fori_loop(1, n_out, lambda k, c: (act(k, lax.rem(me_out + k, n_out)), c)[1], 0)

    def greet(*place):
        pl.semaphore_signal(barrier, inc=1, device_id=place, device_id_type=MESH)

    each_near(lambda k, i: greet(me_out, i))
    each_far(lambda k, o: greet(o, me_in))

    def near_copy(phase, k, source, target, i):
        return pltpu.make_async_remote_copy(
            src_ref=source, dst_ref=target, send_sem=send_sem.at[phase, k], recv_sem=recv_sem.at[phase, k],
            device_id=(me_out, i), device_id_type=MESH,
        )

    def far_copy(phase, k, source, target, o):
        return pltpu.make_async_remote_copy(
            src_ref=source, dst_ref=target, send_sem=send_sem.at[phase, k], recv_sem=recv_sem.at[phase, k],
            device_id=(o, me_in), device_id_type=MESH,
        )

    own_rows = w_ref.shape[0]
    tile = w_near.shape[1]
    per_tile = tile // own_rows
    own_w = jnp.concatenate([w_ref[...].astype(F32)] * per_tile, axis=0)
    own_w = jnp.where(iota(own_w.shape, 0) // own_rows == lax.rem(me_in, per_tile), own_w, 0.0)
    w_near[me_in] = own_w

    pl.semaphore_wait(barrier, n_in + n_out - 2)
    each_near(lambda k, i: near_copy(W_NEAR, k, w_near.at[me_in], w_near.at[me_in], i).start())

    decay = decay_ref[...]
    causal = (iota((rows, rows), 0) >= iota((rows, rows), 1)).astype(F32)
    running = lax.dot_general(causal, decay, NN, precision=HIGH, preferred_element_type=F32)
    total = running[rows - 1:rows, :]
    dt = dt_ref[...]
    to_end = dt * jnp.exp(total - running)
    from_start = jnp.exp(running)
    shifted = running - jnp.log(dt)
    running_t = jnp.transpose(
        jnp.concatenate([running, jnp.zeros((rows, 128 - heads), F32)], axis=1)
    )

    each_near(lambda k, i: near_copy(W_NEAR, k, w_near.at[me_in], w_near.at[lax.rem(me_in + n_in - k, n_in)], i).wait_recv())
    block = [
        functools.reduce(lambda a, b: a + b, [w_near[t * per_tile + q] for q in range(per_tile)])
        for t in range(n_in // per_tile)
    ]
    w_far[me_out] = jnp.concatenate(block, axis=0).astype(BF16)
    each_far(lambda k, o: far_copy(W_FAR, k, w_far.at[me_out], w_far.at[me_out], o).start())

    stack = jnp.concatenate([to_end, from_start, jnp.broadcast_to(total, (8, heads))], axis=0)
    high = stack.astype(BF16)
    rest = stack - high.astype(F32)
    middle = rest.astype(BF16)
    low = (rest - middle.astype(F32)).astype(BF16)
    stack = jnp.concatenate([high, middle, low], axis=1)
    for load in loads:
        load.wait()
    for c in range(lanes // 256):
        at = slice(c * 256, (c + 1) * 256)
        chosen = lax.rem(iota((3 * heads, 256), 0), heads) == (iota((3 * heads, 256), 1) + c * 256) // size
        wide = dot(stack, jnp.where(chosen, 1.0, 0.0).astype(BF16))
        spread[:, at] = wide[:rows]
        xw_hi[:, at], xw_lo[:, at] = split(x[:, at].astype(F32) * wide[:rows])
        gw_hi[:, at], gw_lo[:, at] = split(gy[:, at].astype(F32) * wide[rows:2 * rows])
        for q in range(max(1, 256 // part)):
            lane = c * 256 + q * part
            cut = min(part, 256)
            s_send[lane // part, 2 * state:, lane % part:lane % part + cut] = wide[2 * rows:, q * part:q * part + cut]

    left = iota((rows, 2 * size), 1) < size
    keep = iota((rows, rows), 0) <= iota((rows, rows), 1)
    form = jnp.zeros((rows, rows), F32)

    def stacked(p):
        g = gy[:, p * 2 * size:(p + 1) * 2 * size]
        zero = jnp.zeros_like(g)
        return jnp.concatenate([jnp.where(left, g, zero), jnp.where(left, zero, g)], axis=0)

    for p in range(pairs):
        products = dot(x[:, p * 2 * size:(p + 1) * 2 * size], stacked(p), NT)
        for q in range(2):
            h = 2 * p + q
            spans = running_t[h:h + 1, :] - shifted[:, h:h + 1]
            factor = jnp.exp(jnp.where(keep, spans, -1e30))
            grow[h] = factor
            form = form + factor * products[:, q * rows:(q + 1) * rows]
    for c in range(width // 128):
        hidden_t[c * 128:(c + 1) * 128, :] = jnp.transpose(hidden[:, c * 128:(c + 1) * 128])

    each_far(lambda k, o: far_copy(W_FAR, k, w_far.at[me_out], w_far.at[lax.rem(me_out + n_out - k, n_out)], o).wait_recv())
    w = w_far[...].reshape(width, 2 * state)
    projected = dot(hidden[...], w)
    projected_t = jnp.transpose(projected)
    proj_hi, proj_lo = split(projected_t)
    b_t = jnp.concatenate([proj_hi[:state], proj_lo[:state]], axis=0)
    c_t = jnp.concatenate([proj_hi[state:], proj_lo[state:]], axis=0)

    def own_part(i):
        at = pl.ds(pl.multiple_of(i * part, part), part)
        forward = dot(b_t, xw_hi[:, at])
        s_send[i, :state, :] = forward[:state] + forward[state:] + dot(b_t[:state], xw_lo[:, at])
        backward = dot(c_t, gw_hi[:, at])
        s_send[i, state:2 * state, :] = backward[:state] + backward[state:] + dot(c_t[:state], gw_lo[:, at])

    def send_part(k, i):
        own_part(i)
        near_copy(S_OUT, k, s_send.at[i], s_recv.at[me_in], i).start()

    each_near(send_part)
    own_part(me_in)
    s_recv[me_in] = s_send[me_in]

    b_rows, c_rows = projected[:, :state], projected[:, state:]
    scores = dot3(b_rows, c_rows, NT)
    for p in range(pairs):
        mixed = jnp.concatenate([grow[2 * p] * scores, grow[2 * p + 1] * scores], axis=1).astype(BF16)
        gx[:, p * 2 * size:(p + 1) * 2 * size] = dot(mixed, stacked(p))
    near_b = dot3(form, c_rows)
    near_c = dot3(jnp.transpose(form), b_rows)

    each_near(lambda k, i: near_copy(S_OUT, k, s_send.at[i], s_recv.at[lax.rem(me_in + n_in - k, n_in)], i).wait_recv())

    totals = [s_recv[k, 2 * state:2 * state + 1, :] for k in range(n_in)]
    after, before = jnp.zeros((1, part), F32), jnp.zeros((1, part), F32)
    ahead, behind = [None] * n_in, [None] * n_in
    for k in range(n_in):
        ahead[k], behind[n_in - 1 - k] = jnp.exp(before), jnp.exp(after)
        before = before + totals[k]
        after = after + totals[n_in - 1 - k]
    steps = [jnp.exp(t) for t in totals]
    forward = jnp.zeros((state, part), F32)
    backward = jnp.zeros((state, part), F32)
    for k in range(n_in):
        prefix[k, :state, :] = forward
        forward = forward * steps[k] + s_recv[k, :state, :]
        b = n_in - 1 - k
        prefix[b, state:, :] = backward
        backward = backward * steps[b] + s_recv[b, state:2 * state, :]
    near_sum[:state] = forward
    near_sum[state:] = backward
    for o in range(n_out):
        o_send[o, :far, :] = near_sum[o * far:(o + 1) * far, :]
        o_send[o, far:, :] = jnp.broadcast_to(before, (8, part))
    each_far(lambda k, o: far_copy(S_FAR, k, o_send.at[o], o_recv.at[me_out], o).start())
    o_recv[me_out] = o_send[me_out]
    each_far(lambda k, o: far_copy(S_FAR, k, o_send.at[o], o_recv.at[lax.rem(me_out + n_out - k, n_out)], o).wait_recv())

    is_forward = me_out < n_out // 2
    held = jnp.zeros((far, part), F32)
    for k in range(n_out):
        at = jnp.where(is_forward, k, n_out - 1 - k)
        o_back[at] = held
        held = held * jnp.exp(o_recv[at, far:far + 1, :]) + o_recv[at, :far, :]
    each_far(lambda k, o: far_copy(S_BACK, k, o_back.at[o], carry.at[me_out], o).start())
    carry[me_out] = o_back[me_out]
    each_far(lambda k, o: far_copy(S_BACK, k, o_back.at[o], carry.at[lax.rem(me_out + n_out - k, n_out)], o).wait_recv())

    carried = carry[...].reshape(2 * state, part)
    for k in range(n_in):
        s_back[k, :state, :] = prefix[k, :state, :] + ahead[k] * carried[:state]
        s_back[k, state:, :] = prefix[k, state:, :] + behind[k] * carried[state:]
    each_near(lambda k, i: near_copy(S_HOME, k, s_back.at[i], s_home.at[me_in], i).start())
    s_home[me_in] = s_back[me_in]

    def use_part(i, sums):
        sum_b, sum_c = sums
        at = pl.ds(pl.multiple_of(i * part, part), part)
        got = s_home[i]
        got_hi, got_lo = split(got)
        for_c = jnp.concatenate([got_hi[:state], got_lo[:state]], axis=0)
        for_b = jnp.concatenate([got_hi[state:], got_lo[state:]], axis=0)
        wide_b, wide_c = dot(xw_hi[:, at], for_b, NT), dot(gw_hi[:, at], for_c, NT)
        sum_b = sum_b + wide_b[:, :state] + wide_b[:, state:] + dot(xw_lo[:, at], got_hi[state:], NT)
        sum_c = sum_c + wide_c[:, :state] + wide_c[:, state:] + dot(gw_lo[:, at], got_hi[:state], NT)
        return sum_b, sum_c

    def use_arrived(k, sums):
        i = lax.rem(me_in + n_in - k, n_in)
        near_copy(S_HOME, k, s_back.at[i], s_home.at[i], i).wait_recv()
        return use_part(i, sums)

    sums = use_part(me_in, (near_b, near_c))
    sums = lax.fori_loop(1, n_in, use_arrived, sums)
    d_low = jnp.concatenate(sums, axis=1).astype(BF16)

    cut = width // n_out
    for o in range(n_out):
        g_send[o] = (dot(hidden_t[o * cut:(o + 1) * cut, :], d_low) * scale).astype(BF16)
    each_far(lambda k, o: far_copy(G_FAR, k, g_send.at[o], g_recv.at[me_out], o).start())
    g_recv[me_out] = g_send[me_out]

    gh[...] = dot(d_low, w, NT)
    store_gh = pltpu.make_async_copy(gh, gh_hbm, load_sem.at[0])
    store_gh.start()

    each_far(lambda k, o: far_copy(G_FAR, k, g_send.at[o], g_recv.at[lax.rem(me_out + n_out - k, n_out)], o).wait_recv())
    g_sum[...] = functools.reduce(lambda a, b: a + b, [g_recv[o].astype(F32) for o in range(n_out)])

    def owned(i):
        return g_sum.at[pl.ds(pl.multiple_of(i // per_tile * tile, tile), tile), :]

    each_near(lambda k, i: near_copy(G_NEAR, k, owned(i), g_near.at[me_in], i).start())
    g_near[me_in] = g_sum[pl.ds(pl.multiple_of(me_in // per_tile * tile, tile), tile), :]

    b_hi, b_lo = split(b_rows)
    b_three = jnp.concatenate([b_hi, b_lo, b_hi], axis=1)
    for i in range(n_in):
        at = slice(i * part, (i + 1) * part)
        got_hi, got_lo = split(s_home[i, state:, :])
        gx[:, at] = gx[:, at] + spread[:, at] * dot(b_three, jnp.concatenate([got_hi, got_hi, got_lo], axis=0))
    store_gx = pltpu.make_async_copy(gx, gx_hbm, load_sem.at[1])
    store_gx.start()

    each_near(lambda k, i: near_copy(G_NEAR, k, owned(i), g_near.at[lax.rem(me_in + n_in - k, n_in)], i).wait_recv())
    summed = functools.reduce(lambda a, b: a + b, [g_near[i] for i in range(n_in)])
    mine = summed[:own_rows]
    for q in range(1, per_tile):
        mine = jnp.where(lax.rem(me_in, per_tile) == q, summed[q * own_rows:(q + 1) * own_rows], mine)
    gp_ref[...] = mine

    each_near(lambda k, i: near_copy(W_NEAR, k, w_near.at[me_in], w_near.at[me_in], i).wait_send())
    each_far(lambda k, o: far_copy(W_FAR, k, w_far.at[me_out], w_far.at[me_out], o).wait_send())
    each_near(lambda k, i: near_copy(S_OUT, k, s_send.at[i], s_recv.at[me_in], i).wait_send())
    each_far(lambda k, o: far_copy(S_FAR, k, o_send.at[o], o_recv.at[me_out], o).wait_send())
    each_far(lambda k, o: far_copy(S_BACK, k, o_back.at[o], carry.at[me_out], o).wait_send())
    each_near(lambda k, i: near_copy(S_HOME, k, s_back.at[i], s_home.at[me_in], i).wait_send())
    each_far(lambda k, o: far_copy(G_FAR, k, g_send.at[o], g_recv.at[me_out], o).wait_send())
    each_near(lambda k, i: near_copy(G_NEAR, k, owned(i), g_near.at[me_in], i).wait_send())
    store_gh.wait()
    store_gx.wait()


def per_device(hidden, x_act, dt_step, log_decay, w_bc, grad_y):
    n_out, n_in = lax.axis_size("outer"), lax.axis_size("inner")
    rows, width = hidden.shape
    lanes = x_act.shape[1]
    heads = dt_step.shape[1]
    own_rows, columns = w_bc.shape
    part = lanes // n_in
    far = columns // n_out
    tile = max(8, own_rows)
    most = max(n_out, n_in)
    scale = 1.0 / math.sqrt(rows * n_out * n_in)
    anywhere = pl.BlockSpec(memory_space=pl.ANY)
    vmem = pl.BlockSpec(memory_space=pltpu.VMEM)
    return pl.pallas_call(
        functools.partial(kernel, scale, n_out, n_in),
        out_shape=(
            jax.ShapeDtypeStruct((rows, lanes), F32),
            jax.ShapeDtypeStruct((rows, width), F32),
            jax.ShapeDtypeStruct((own_rows, columns), F32),
        ),
        in_specs=[anywhere, anywhere, vmem, vmem, vmem, anywhere],
        out_specs=(anywhere, anywhere, vmem),
        scratch_shapes=[
            pltpu.VMEM((rows, width), BF16),
            pltpu.VMEM((rows, lanes), BF16),
            pltpu.VMEM((rows, lanes), BF16),
            pltpu.VMEM((width, rows), BF16),
            pltpu.VMEM((rows, lanes), F32),
            pltpu.VMEM((rows, width), F32),
            pltpu.VMEM((n_in, tile, columns), F32),
            pltpu.VMEM((n_out, width // n_out, columns), BF16),
            pltpu.VMEM((heads, rows, rows), F32),
            pltpu.VMEM((rows, lanes), F32),
            pltpu.VMEM((rows, lanes), BF16),
            pltpu.VMEM((rows, lanes), BF16),
            pltpu.VMEM((rows, lanes), BF16),
            pltpu.VMEM((rows, lanes), BF16),
            pltpu.VMEM((n_in, columns + 8, part), F32),
            pltpu.VMEM((n_in, columns + 8, part), F32),
            pltpu.VMEM((n_in, columns, part), F32),
            pltpu.VMEM((columns, part), F32),
            pltpu.VMEM((n_out, far + 8, part), F32),
            pltpu.VMEM((n_out, far + 8, part), F32),
            pltpu.VMEM((n_out, far, part), F32),
            pltpu.VMEM((n_out, far, part), F32),
            pltpu.VMEM((n_in, columns, part), F32),
            pltpu.VMEM((n_in, columns, part), F32),
            pltpu.VMEM((n_out, width // n_out, columns), BF16),
            pltpu.VMEM((n_out, width // n_out, columns), BF16),
            pltpu.VMEM((width // n_out, columns), F32),
            pltpu.VMEM((n_in, tile, columns), F32),
            pltpu.SemaphoreType.DMA((3,)),
            pltpu.SemaphoreType.DMA((8, most)),
            pltpu.SemaphoreType.DMA((8, most)),
        ],
        compiler_params=pltpu.CompilerParams(
            collective_id=0, has_side_effects=True, vmem_limit_bytes=48 * 1024 * 1024
        ),
        cost_estimate=pl.CostEstimate(flops=10**9, bytes_accessed=3 * 10**6, transcendentals=10**6),
    )(hidden, x_act, dt_step, log_decay, w_bc, grad_y)


def solution(mesh):
    spec = P(("outer", "inner"), None)
    return jax.shard_map(
        per_device, mesh=mesh, in_specs=(spec,) * 6, out_specs=(spec,) * 3, check_vma=False
    )
```

```python
import functools
import math

import jax
import jax.numpy as jnp
from jax import lax
from jax.experimental import pallas as pl
from jax.experimental.pallas import tpu as pltpu
from jax.sharding import PartitionSpec as P

BF16 = jnp.bfloat16
F32 = jnp.float32
MESH = pl.DeviceIdType.MESH
HIGH = lax.Precision.HIGHEST

NN = (((1,), (0,)), ((), ()))
NT = (((1,), (1,)), ((), ()))

W_NEAR, W_FAR, S_FAR, S_BACK, G_FAR, G_NEAR, S_OUT = range(7)
PIECES = 2
S_HOME = S_OUT + PIECES
PHASES = S_HOME + PIECES


def dot(a, b, dims=NN):
    return lax.dot_general(a, b, dims, preferred_element_type=F32)


def split(value):
    high = value.astype(BF16)
    return high, (value - high.astype(F32)).astype(BF16)


def dot3(a, b, dims=NN):
    a_high, a_low = split(a)
    b_high, b_low = split(b)
    return dot(a_high, b_high, dims) + dot(a_high, b_low, dims) + dot(a_low, b_high, dims)


def iota(shape, axis):
    return lax.broadcasted_iota(jnp.int32, shape, axis)


def kernel(
    scale, n_out, n_in,
    hidden_hbm, x_hbm, dt_hbm, decay_hbm, w_ref, gy_hbm,
    gx_hbm, gh_hbm, gp_ref,
    hidden, x, gy, dt_ref, decay_ref, hidden_t, gx, gh,
    w_near, w_far, grow, spread, xw_hi, xw_lo, gw_hi, gw_lo,
    s_send, s_recv, prefix, o_send, o_recv, o_back, carry, s_back, s_home,
    g_send, g_recv, g_sum, g_near,
    load_sem, send_sem, recv_sem,
):
    me_out, me_in = lax.axis_index("outer"), lax.axis_index("inner")
    rows, width = hidden.shape
    lanes = x.shape[1]
    heads = dt_ref.shape[0]
    size = lanes // heads
    state = w_far.shape[2] // 2
    part = lanes // n_in
    far = 2 * state // n_out
    pairs = heads // 2

    loads = [
        pltpu.make_async_copy(source, target, load_sem.at[k])
        for k, (source, target) in enumerate(
            ((decay_hbm, decay_ref), (dt_hbm, dt_ref), (x_hbm, x), (gy_hbm, gy), (hidden_hbm, hidden))
        )
    ]
    for load in loads:
        load.start()

    barrier = pltpu.get_barrier_semaphore()

    def each_near(act):
        lax.fori_loop(1, n_in, lambda k, c: (act(k, lax.rem(me_in + k, n_in)), c)[1], 0)

    def each_far(act):
        lax.fori_loop(1, n_out, lambda k, c: (act(k, lax.rem(me_out + k, n_out)), c)[1], 0)

    def greet(*place):
        pl.semaphore_signal(barrier, inc=1, device_id=place, device_id_type=MESH)

    each_near(lambda k, i: greet(me_out, i))
    each_far(lambda k, o: greet(o, me_in))

    def near_copy(phase, k, source, target, i):
        return pltpu.make_async_remote_copy(
            src_ref=source, dst_ref=target, send_sem=send_sem.at[phase, k], recv_sem=recv_sem.at[phase, k],
            device_id=(me_out, i), device_id_type=MESH,
        )

    def far_copy(phase, k, source, target, o):
        return pltpu.make_async_remote_copy(
            src_ref=source, dst_ref=target, send_sem=send_sem.at[phase, k], recv_sem=recv_sem.at[phase, k],
            device_id=(o, me_in), device_id_type=MESH,
        )

    own_rows = w_ref.shape[0]
    tile = w_near.shape[1]
    per_tile = tile // own_rows
    own_w = jnp.concatenate([w_ref[...].astype(F32)] * per_tile, axis=0)
    own_w = jnp.where(iota(own_w.shape, 0) // own_rows == lax.rem(me_in, per_tile), own_w, 0.0)
    w_near[me_in] = own_w

    pl.semaphore_wait(barrier, n_in + n_out - 2)
    each_near(lambda k, i: near_copy(W_NEAR, k, w_near.at[me_in], w_near.at[me_in], i).start())

    loads[0].wait()
    loads[1].wait()
    upto = (iota((rows, rows), 0) <= iota((rows, rows), 1)).astype(F32)
    running_t = lax.dot_general(decay_ref[...], upto, NN, precision=HIGH, preferred_element_type=F32)
    dt_t = dt_ref[...]
    total_t = jnp.broadcast_to(running_t[:, rows - 1:], running_t.shape)
    columns = jnp.transpose(jnp.concatenate(
        [dt_t * jnp.exp(total_t - running_t), jnp.exp(running_t), total_t, running_t - jnp.log(dt_t)], axis=0
    ))
    shifted = columns[:, 3 * heads:]
    stack = jnp.concatenate(
        [columns[:, :heads], columns[:, heads:2 * heads], columns[:8, 2 * heads:3 * heads]], axis=0
    )
    high = stack.astype(BF16)
    rest = stack - high.astype(F32)
    middle = rest.astype(BF16)
    low = (rest - middle.astype(F32)).astype(BF16)
    stack = jnp.concatenate([high, middle, low], axis=1)
    for load in loads[2:]:
        load.wait()
    for c in range(lanes // 256):
        at = slice(c * 256, (c + 1) * 256)
        chosen = lax.rem(iota((3 * heads, 256), 0), heads) == (iota((3 * heads, 256), 1) + c * 256) // size
        wide = dot(stack, jnp.where(chosen, 1.0, 0.0).astype(BF16))
        spread[:, at] = wide[:rows]
        xw_hi[:, at], xw_lo[:, at] = split(x[:, at].astype(F32) * wide[:rows])
        gw_hi[:, at], gw_lo[:, at] = split(gy[:, at].astype(F32) * wide[rows:2 * rows])
        for q in range(max(1, 256 // part)):
            lane = c * 256 + q * part
            cut = min(part, 256)
            s_send[lane // part, :8, lane % part:lane % part + cut] = wide[2 * rows:, q * part:q * part + cut]

    each_near(lambda k, i: near_copy(W_NEAR, k, w_near.at[me_in], w_near.at[lax.rem(me_in + n_in - k, n_in)], i).wait_recv())
    block = [
        functools.reduce(lambda a, b: a + b, [w_near[t * per_tile + q] for q in range(per_tile)])
        for t in range(n_in // per_tile)
    ]
    w_far[me_out] = jnp.concatenate(block, axis=0).astype(BF16)
    each_far(lambda k, o: far_copy(W_FAR, k, w_far.at[me_out], w_far.at[me_out], o).start())

    left = iota((rows, 2 * size), 1) < size
    keep = iota((rows, rows), 0) <= iota((rows, rows), 1)
    form = jnp.zeros((rows, rows), F32)

    def stacked(p):
        g = gy[:, p * 2 * size:(p + 1) * 2 * size]
        zero = jnp.zeros_like(g)
        return jnp.concatenate([jnp.where(left, g, zero), jnp.where(left, zero, g)], axis=0)

    for p in range(pairs):
        products = dot(x[:, p * 2 * size:(p + 1) * 2 * size], stacked(p), NT)
        for q in range(2):
            h = 2 * p + q
            spans = running_t[h:h + 1, :] - shifted[:, h:h + 1]
            factor = jnp.exp(jnp.where(keep, spans, -1e30))
            grow[h] = factor
            form = form + factor * products[:, q * rows:(q + 1) * rows]
    for c in range(width // 128):
        hidden_t[c * 128:(c + 1) * 128, :] = jnp.transpose(hidden[:, c * 128:(c + 1) * 128])

    each_far(lambda k, o: far_copy(W_FAR, k, w_far.at[me_out], w_far.at[lax.rem(me_out + n_out - k, n_out)], o).wait_recv())
    w = w_far[...].reshape(width, 2 * state)
    projected = dot(hidden[...], w)
    projected_t = jnp.transpose(projected)
    proj_hi, proj_lo = split(projected_t)
    b_t = jnp.concatenate([proj_hi[:state], proj_lo[:state]], axis=0)
    c_t = jnp.concatenate([proj_hi[state:], proj_lo[state:]], axis=0)

    step = 2 * state // PIECES

    def rows_of(q):
        return slice(8 + q * step if q else 0, 8 + (q + 1) * step)

    def own_part(q, i):
        at = pl.ds(pl.multiple_of(i * part, part), part)
        which = b_t if q == 0 else c_t
        values, rests = (xw_hi, xw_lo) if q == 0 else (gw_hi, gw_lo)
        both = dot(which, values[:, at])
        s_send[i, 8 + q * state:8 + (q + 1) * state, :] = both[:state] + both[state:] + dot(which[:state], rests[:, at])

    def out_copy(q, k, source, i):
        return near_copy(S_OUT + q, k, s_send.at[i, rows_of(q)], s_recv.at[source, rows_of(q)], i)

    half = PIECES // 2
    for way in range(2):
        def send_part(k, i, way=way):
            own_part(way, i)
            for q in range(way * half, (way + 1) * half):
                out_copy(q, k, me_in, i).start()

        each_near(send_part)
        own_part(way, me_in)
    s_recv[me_in] = s_send[me_in]

    b_rows, c_rows = projected[:, :state], projected[:, state:]
    scores = dot3(b_rows, c_rows, NT)
    for p in range(pairs):
        mixed = jnp.concatenate([grow[2 * p] * scores, grow[2 * p + 1] * scores], axis=1).astype(BF16)
        gx[:, p * 2 * size:(p + 1) * 2 * size] = dot(mixed, stacked(p))
    near_b = dot3(form, c_rows)
    near_c = dot3(jnp.transpose(form), b_rows)

    servers = n_out // PIECES

    def far_send(q, k, o):
        @pl.when(o // servers == q)
        def _():
            far_copy(S_FAR, k, o_send.at[o], o_recv.at[me_out], o).start()

    def far_step(forward):
        o_recv[me_out] = o_send[me_out]
        each_far(lambda k, o: far_copy(S_FAR, k, o_send.at[o], o_recv.at[lax.rem(me_out + n_out - k, n_out)], o).wait_recv())
        held = jnp.zeros((far, part), F32)
        for k in range(n_out):
            at = k if forward else n_out - 1 - k
            o_back[at] = held
            held = held * jnp.exp(o_recv[at, far:far + 1, :]) + o_recv[at, :far, :]
        each_far(lambda k, o: far_copy(S_BACK, k, o_back.at[o], carry.at[me_out], o).start())
        carry[me_out] = o_back[me_out]

    for q in range(PIECES):
        forward = q < half
        each_near(lambda k, i: out_copy(q, k, lax.rem(me_in + n_in - k, n_in), i).wait_recv())
        if q == 0:
            totals = [s_recv[k, :1, :] for k in range(n_in)]
            after, before = jnp.zeros((1, part), F32), jnp.zeros((1, part), F32)
            ahead, behind = [None] * n_in, [None] * n_in
            for k in range(n_in):
                ahead[k], behind[n_in - 1 - k] = jnp.exp(before), jnp.exp(after)
                before = before + totals[k]
                after = after + totals[n_in - 1 - k]
            steps = [jnp.exp(t) for t in totals]
        held = jnp.zeros((step, part), F32)
        for k in range(n_in) if forward else range(n_in - 1, -1, -1):
            prefix[k, q * step:(q + 1) * step, :] = held
            held = held * steps[k] + s_recv[k, 8 + q * step:8 + (q + 1) * step, :]
        for j in range(servers):
            o_send[q * servers + j, :far, :] = held[j * far:(j + 1) * far]
            o_send[q * servers + j, far:, :] = jnp.broadcast_to(before, (8, part))
        each_far(functools.partial(far_send, q))

    for forward in (True, False):
        pl.when((me_out < n_out // 2) == forward)(functools.partial(far_step, forward))

    def back_wait(q, k, o):
        source = lax.rem(me_out + n_out - k, n_out)

        @pl.when(source // servers == q)
        def _():
            far_copy(S_BACK, k, o_back.at[o], carry.at[source], o).wait_recv()

    def home_copy(q, k, source, i):
        at = slice(q * step, (q + 1) * step)
        return near_copy(S_HOME + q, k, s_back.at[i, at], s_home.at[source, at], i)

    for q in range(PIECES):
        each_far(functools.partial(back_wait, q))
        carried = jnp.concatenate([carry[q * servers + j] for j in range(servers)], axis=0)
        reach = ahead if q < half else behind
        at = slice(q * step, (q + 1) * step)
        for k in range(n_in):
            s_back[k, at, :] = prefix[k, at, :] + reach[k] * carried
        each_near(lambda k, i: home_copy(q, k, me_in, i).start())
    s_home[me_in] = s_back[me_in]

    def use_part(way, i, sum_):
        at = pl.ds(pl.multiple_of(i * part, part), part)
        values, rests = (gw_hi, gw_lo) if way == 0 else (xw_hi, xw_lo)
        got_hi, got_lo = split(s_home[i, way * state:(way + 1) * state, :])
        both = dot(values[:, at], jnp.concatenate([got_hi, got_lo], axis=0), NT)
        return sum_ + both[:, :state] + both[:, state:] + dot(rests[:, at], got_hi, NT)

    sums = []
    for way, near in enumerate((near_c, near_b)):
        def use_arrived(k, sum_, way=way):
            i = lax.rem(me_in + n_in - k, n_in)
            for q in range(way * half, (way + 1) * half):
                home_copy(q, k, i, i).wait_recv()
            return use_part(way, i, sum_)

        sums.append(lax.fori_loop(1, n_in, use_arrived, use_part(way, me_in, near)))
    sums = sums[::-1]
    d_low = jnp.concatenate(sums, axis=1).astype(BF16)

    cut = width // n_out
    for o in range(n_out):
        g_send[o] = (dot(hidden_t[o * cut:(o + 1) * cut, :], d_low) * scale).astype(BF16)
    each_far(lambda k, o: far_copy(G_FAR, k, g_send.at[o], g_recv.at[me_out], o).start())
    g_recv[me_out] = g_send[me_out]

    gh[...] = dot(d_low, w, NT)
    store_gh = pltpu.make_async_copy(gh, gh_hbm, load_sem.at[0])
    store_gh.start()

    each_far(lambda k, o: far_copy(G_FAR, k, g_send.at[o], g_recv.at[lax.rem(me_out + n_out - k, n_out)], o).wait_recv())
    g_sum[...] = functools.reduce(lambda a, b: a + b, [g_recv[o].astype(F32) for o in range(n_out)])

    def owned(i):
        return g_sum.at[pl.ds(pl.multiple_of(i // per_tile * tile, tile), tile), :]

    each_near(lambda k, i: near_copy(G_NEAR, k, owned(i), g_near.at[me_in], i).start())
    g_near[me_in] = g_sum[pl.ds(pl.multiple_of(me_in // per_tile * tile, tile), tile), :]

    b_hi, b_lo = split(b_rows)
    b_three = jnp.concatenate([b_hi, b_lo, b_hi], axis=1)
    for i in range(n_in):
        at = slice(i * part, (i + 1) * part)
        got_hi, got_lo = split(s_home[i, state:, :])
        gx[:, at] = gx[:, at] + spread[:, at] * dot(b_three, jnp.concatenate([got_hi, got_hi, got_lo], axis=0))
    store_gx = pltpu.make_async_copy(gx, gx_hbm, load_sem.at[1])
    store_gx.start()

    each_near(lambda k, i: near_copy(G_NEAR, k, owned(i), g_near.at[lax.rem(me_in + n_in - k, n_in)], i).wait_recv())
    summed = functools.reduce(lambda a, b: a + b, [g_near[i] for i in range(n_in)])
    mine = summed[:own_rows]
    for q in range(1, per_tile):
        mine = jnp.where(lax.rem(me_in, per_tile) == q, summed[q * own_rows:(q + 1) * own_rows], mine)
    gp_ref[...] = mine

    each_near(lambda k, i: near_copy(W_NEAR, k, w_near.at[me_in], w_near.at[me_in], i).wait_send())
    each_far(lambda k, o: far_copy(W_FAR, k, w_far.at[me_out], w_far.at[me_out], o).wait_send())
    for q in range(PIECES):
        each_near(lambda k, i: out_copy(q, k, me_in, i).wait_send())
        each_near(lambda k, i: home_copy(q, k, me_in, i).wait_send())
    each_far(lambda k, o: far_copy(S_FAR, k, o_send.at[o], o_recv.at[me_out], o).wait_send())
    each_far(lambda k, o: far_copy(S_BACK, k, o_back.at[o], carry.at[me_out], o).wait_send())
    each_far(lambda k, o: far_copy(G_FAR, k, g_send.at[o], g_recv.at[me_out], o).wait_send())
    each_near(lambda k, i: near_copy(G_NEAR, k, owned(i), g_near.at[me_in], i).wait_send())
    store_gh.wait()
    store_gx.wait()


def write_out(gx_from, gh_from, gp_from, gx_to, gh_to, gp_to, gx, gh, gp, sem):
    pieces = gx.shape[1]
    moves = [(gp_from, gp, gp_to)]
    for q in range(gx.shape[0]):
        at = slice(q * pieces, (q + 1) * pieces)
        moves.append((gx_from.at[at], gx.at[q], gx_to.at[at]))
        moves.append((gh_from.at[at], gh.at[q], gh_to.at[at]))
    reads = [pltpu.make_async_copy(m[0], m[1], sem.at[0, k]) for k, m in enumerate(moves)]
    writes = [pltpu.make_async_copy(m[1], m[2], sem.at[1, k]) for k, m in enumerate(moves)]
    for read in reads:
        read.start()
    for read, write in zip(reads, writes):
        read.wait()
        write.start()
    for write in writes:
        write.wait()


def per_device(hidden, x_act, dt_step, log_decay, w_bc, grad_y):
    n_out, n_in = lax.axis_size("outer"), lax.axis_size("inner")
    rows, width = hidden.shape
    lanes = x_act.shape[1]
    heads = dt_step.shape[1]
    own_rows, columns = w_bc.shape
    part = lanes // n_in
    far = columns // n_out
    tile = max(8, own_rows)
    most = max(n_out, n_in)
    scale = 1.0 / math.sqrt(rows * n_out * n_in)
    anywhere = pl.BlockSpec(memory_space=pl.ANY)
    vmem = pl.BlockSpec(memory_space=pltpu.VMEM)
    results = pl.pallas_call(
        functools.partial(kernel, scale, n_out, n_in),
        out_shape=(
            jax.ShapeDtypeStruct((rows, lanes), F32),
            jax.ShapeDtypeStruct((rows, width), F32),
            jax.ShapeDtypeStruct((own_rows, columns), F32),
        ),
        in_specs=[anywhere, anywhere, anywhere, anywhere, vmem, anywhere],
        out_specs=(anywhere, anywhere, vmem),
        scratch_shapes=[
            pltpu.VMEM((rows, width), BF16),
            pltpu.VMEM((rows, lanes), BF16),
            pltpu.VMEM((rows, lanes), BF16),
            pltpu.VMEM((heads, rows), F32),
            pltpu.VMEM((heads, rows), F32),
            pltpu.VMEM((width, rows), BF16),
            pltpu.VMEM((rows, lanes), F32),
            pltpu.VMEM((rows, width), F32),
            pltpu.VMEM((n_in, tile, columns), F32),
            pltpu.VMEM((n_out, width // n_out, columns), BF16),
            pltpu.VMEM((heads, rows, rows), F32),
            pltpu.VMEM((rows, lanes), F32),
            pltpu.VMEM((rows, lanes), BF16),
            pltpu.VMEM((rows, lanes), BF16),
            pltpu.VMEM((rows, lanes), BF16),
            pltpu.VMEM((rows, lanes), BF16),
            pltpu.VMEM((n_in, columns + 8, part), F32),
            pltpu.VMEM((n_in, columns + 8, part), F32),
            pltpu.VMEM((n_in, columns, part), F32),
            pltpu.VMEM((n_out, far + 8, part), F32),
            pltpu.VMEM((n_out, far + 8, part), F32),
            pltpu.VMEM((n_out, far, part), F32),
            pltpu.VMEM((n_out, far, part), F32),
            pltpu.VMEM((n_in, columns, part), F32),
            pltpu.VMEM((n_in, columns, part), F32),
            pltpu.VMEM((n_out, width // n_out, columns), BF16),
            pltpu.VMEM((n_out, width // n_out, columns), BF16),
            pltpu.VMEM((width // n_out, columns), F32),
            pltpu.VMEM((n_in, tile, columns), F32),
            pltpu.SemaphoreType.DMA((5,)),
            pltpu.SemaphoreType.DMA((PHASES, most)),
            pltpu.SemaphoreType.DMA((PHASES, most)),
        ],
        compiler_params=pltpu.CompilerParams(
            collective_id=0, has_side_effects=True, vmem_limit_bytes=60 * 1024 * 1024
        ),
        cost_estimate=pl.CostEstimate(flops=10**9, bytes_accessed=3 * 10**6, transcendentals=10**6),
    )(hidden, x_act, dt_step.T, log_decay.T, w_bc, grad_y)
    pieces = rows // 4
    return pl.pallas_call(
        write_out,
        out_shape=tuple(jax.ShapeDtypeStruct(r.shape, r.dtype) for r in results),
        in_specs=[anywhere] * 3,
        out_specs=(anywhere,) * 3,
        scratch_shapes=[
            pltpu.VMEM((4, pieces, lanes), F32),
            pltpu.VMEM((4, pieces, width), F32),
            pltpu.VMEM((own_rows, columns), F32),
            pltpu.SemaphoreType.DMA((2, 9)),
        ],
        compiler_params=pltpu.CompilerParams(vmem_limit_bytes=60 * 1024 * 1024),
    )(*results)


def solution(mesh):
    spec = P(("outer", "inner"), None)
    return jax.shard_map(
        per_device, mesh=mesh, in_specs=(spec,) * 6, out_specs=(spec,) * 3, check_vma=False
    )
```

```python
import functools
import math

import jax
import jax.numpy as jnp
from jax import lax
from jax.experimental import pallas as pl
from jax.experimental.pallas import tpu as pltpu
from jax.sharding import PartitionSpec as P

BF16 = jnp.bfloat16
F32 = jnp.float32
MESH = pl.DeviceIdType.MESH
HIGH = lax.Precision.HIGHEST

NN = (((1,), (0,)), ((), ()))
NT = (((1,), (1,)), ((), ()))

W_NEAR, W_FAR, S_FAR, S_BACK, G_FAR, G_NEAR, S_OUT = range(7)
WAYS = 2
S_HOME = S_OUT + WAYS
C_OUT = S_HOME + WAYS
C_HOME = C_OUT + WAYS
PHASES = C_HOME + WAYS


def dot(a, b, dims=NN):
    return lax.dot_general(a, b, dims, preferred_element_type=F32)


def split(value):
    high = value.astype(BF16)
    return high, (value - high.astype(F32)).astype(BF16)


def dot3(a, b, dims=NN):
    a_high, a_low = split(a)
    b_high, b_low = split(b)
    return dot(a_high, b_high, dims) + dot(a_high, b_low, dims) + dot(a_low, b_high, dims)


def iota(shape, axis):
    return lax.broadcasted_iota(jnp.int32, shape, axis)


def kernel(
    scale, n_out, n_in,
    hidden_hbm, x_hbm, dt_hbm, decay_hbm, w_ref, gy_hbm,
    gx_hbm, gh_hbm, gp_ref,
    hidden, x, gy, dt_ref, decay_ref, hidden_t, gx, gh,
    w_near, w_far, grow, spread, xw_hi, xw_lo, gw_hi, gw_lo,
    c_send, c_recv, s_send, s_recv, prefix, o_send, o_recv, o_back, carry, s_back, s_home, c_back, states,
    g_send, g_recv, g_sum, g_near,
    load_sem, send_sem, recv_sem,
):
    me_out, me_in = lax.axis_index("outer"), lax.axis_index("inner")
    rows, width = hidden.shape
    lanes = x.shape[1]
    heads = dt_ref.shape[0]
    size = lanes // heads
    state = w_far.shape[2] // 2
    part = lanes // n_in
    far = 2 * state // n_out
    pairs = heads // 2
    n_chip = n_in // 2
    chip, core = me_in // 2, lax.rem(me_in, 2)
    other = 1 - core

    loads = [
        pltpu.make_async_copy(source, target, load_sem.at[k])
        for k, (source, target) in enumerate(
            ((decay_hbm, decay_ref), (dt_hbm, dt_ref), (x_hbm, x), (gy_hbm, gy), (hidden_hbm, hidden))
        )
    ]
    for load in loads:
        load.start()

    barrier = pltpu.get_barrier_semaphore()

    def each_near(act):
        lax.fori_loop(1, n_in, lambda k, c: (act(k, lax.rem(me_in + k, n_in)), c)[1], 0)

    def each_chip(act):
        lax.fori_loop(1, n_chip, lambda k, c: (act(k, lax.rem(chip + k, n_chip)), c)[1], 0)

    def each_far(act):
        lax.fori_loop(1, n_out, lambda k, c: (act(k, lax.rem(me_out + k, n_out)), c)[1], 0)

    def greet(*place):
        pl.semaphore_signal(barrier, inc=1, device_id=place, device_id_type=MESH)

    each_near(lambda k, i: greet(me_out, i))
    each_far(lambda k, o: greet(o, me_in))

    def near_copy(phase, k, source, target, i):
        return pltpu.make_async_remote_copy(
            src_ref=source, dst_ref=target, send_sem=send_sem.at[phase, k], recv_sem=recv_sem.at[phase, k],
            device_id=(me_out, i), device_id_type=MESH,
        )

    def far_copy(phase, k, source, target, o):
        return pltpu.make_async_remote_copy(
            src_ref=source, dst_ref=target, send_sem=send_sem.at[phase, k], recv_sem=recv_sem.at[phase, k],
            device_id=(o, me_in), device_id_type=MESH,
        )

    own_rows = w_ref.shape[0]
    tile = w_near.shape[1]
    per_tile = tile // own_rows
    own_w = jnp.concatenate([w_ref[...].astype(F32)] * per_tile, axis=0)
    own_w = jnp.where(iota(own_w.shape, 0) // own_rows == lax.rem(me_in, per_tile), own_w, 0.0)
    w_near[me_in] = own_w

    pl.semaphore_wait(barrier, n_in + n_out - 2)
    each_near(lambda k, i: near_copy(W_NEAR, k, w_near.at[me_in], w_near.at[me_in], i).start())

    loads[0].wait()
    loads[1].wait()
    upto = (iota((rows, rows), 0) <= iota((rows, rows), 1)).astype(F32)
    running_t = lax.dot_general(decay_ref[...], upto, NN, precision=HIGH, preferred_element_type=F32)
    dt_t = dt_ref[...]
    total_t = jnp.broadcast_to(running_t[:, rows - 1:], running_t.shape)
    columns = jnp.transpose(jnp.concatenate(
        [dt_t * jnp.exp(total_t - running_t), jnp.exp(running_t), total_t, running_t - jnp.log(dt_t)], axis=0
    ))
    shifted = columns[:, 3 * heads:]
    stack = jnp.concatenate(
        [columns[:, :heads], columns[:, heads:2 * heads], columns[:8, 2 * heads:3 * heads]], axis=0
    )
    high = stack.astype(BF16)
    rest = stack - high.astype(F32)
    middle = rest.astype(BF16)
    low = (rest - middle.astype(F32)).astype(BF16)
    stack = jnp.concatenate([high, middle, low], axis=1)
    for load in loads[2:]:
        load.wait()
    for c in range(lanes // 256):
        at = slice(c * 256, (c + 1) * 256)
        chosen = lax.rem(iota((3 * heads, 256), 0), heads) == (iota((3 * heads, 256), 1) + c * 256) // size
        wide = dot(stack, jnp.where(chosen, 1.0, 0.0).astype(BF16))
        spread[:, at] = wide[:rows]
        xw_hi[:, at], xw_lo[:, at] = split(x[:, at].astype(F32) * wide[:rows])
        gw_hi[:, at], gw_lo[:, at] = split(gy[:, at].astype(F32) * wide[rows:2 * rows])
        for q in range(max(1, 256 // part)):
            lane = c * 256 + q * part
            cut = min(part, 256)
            i = lane // part
            c_send[i % 2, i // 2, :8, lane % part:lane % part + cut] = wide[2 * rows:, q * part:q * part + cut]

    each_near(lambda k, i: near_copy(W_NEAR, k, w_near.at[me_in], w_near.at[lax.rem(me_in + n_in - k, n_in)], i).wait_recv())
    block = [
        functools.reduce(lambda a, b: a + b, [w_near[t * per_tile + q] for q in range(per_tile)])
        for t in range(n_in // per_tile)
    ]
    w_far[me_out] = jnp.concatenate(block, axis=0).astype(BF16)
    each_far(lambda k, o: far_copy(W_FAR, k, w_far.at[me_out], w_far.at[me_out], o).start())

    left = iota((rows, 2 * size), 1) < size
    keep = iota((rows, rows), 0) <= iota((rows, rows), 1)
    form = jnp.zeros((rows, rows), F32)

    def stacked(p):
        g = gy[:, p * 2 * size:(p + 1) * 2 * size]
        zero = jnp.zeros_like(g)
        return jnp.concatenate([jnp.where(left, g, zero), jnp.where(left, zero, g)], axis=0)

    for p in range(pairs):
        products = dot(x[:, p * 2 * size:(p + 1) * 2 * size], stacked(p), NT)
        for q in range(2):
            h = 2 * p + q
            spans = running_t[h:h + 1, :] - shifted[:, h:h + 1]
            factor = jnp.exp(jnp.where(keep, spans, -1e30))
            grow[h] = factor
            form = form + factor * products[:, q * rows:(q + 1) * rows]
    for c in range(width // 128):
        hidden_t[c * 128:(c + 1) * 128, :] = jnp.transpose(hidden[:, c * 128:(c + 1) * 128])

    each_far(lambda k, o: far_copy(W_FAR, k, w_far.at[me_out], w_far.at[lax.rem(me_out + n_out - k, n_out)], o).wait_recv())
    w = w_far[...].reshape(width, 2 * state)
    projected = dot(hidden[...], w)
    projected_t = jnp.transpose(projected)
    proj_hi, proj_lo = split(projected_t)
    b_t = jnp.concatenate([proj_hi[:state], proj_lo[:state]], axis=0)
    c_t = jnp.concatenate([proj_hi[state:], proj_lo[state:]], axis=0)

    def rows_of(way):
        return slice(8 + state, 8 + 2 * state) if way else slice(0, 8 + state)

    def state_rows(way, first=8):
        return slice(first + way * state, first + (way + 1) * state)

    def lanes_of(side, t):
        return pl.ds(pl.multiple_of((t * 2 + side) * part, part), part)

    def own_part(way, side, t):
        at = lanes_of(side, t)
        which = c_t if way else b_t
        values, rests = (gw_hi, gw_lo) if way else (xw_hi, xw_lo)
        both = dot(which, values[:, at])
        c_send[side, t, state_rows(way), :] = both[:state] + both[state:] + dot(which[:state], rests[:, at])

    def core_out(way, k, t):
        return near_copy(C_OUT + way, k, c_send.at[other, t, rows_of(way)], c_recv.at[t, rows_of(way)], chip * 2 + other)

    def chip_out(way, k, t, source):
        return near_copy(S_OUT + way, k, s_send.at[t, rows_of(way)], s_recv.at[source, rows_of(way)], t * 2 + core)

    def each_slice(act):
        lax.fori_loop(1, n_chip + 1, lambda k, c: (act(k, lax.rem(chip + k, n_chip)), c)[1], 0)

    def give(way):
        def one(k, t):
            own_part(way, other, t)
            core_out(way, k, t).start()

        each_slice(one)

    first_core = core == 0

    def join(way):
        def one(k, t):
            core_out(way, k, t).wait_recv()
            own_total, other_total = c_send[core, t, :1, :], c_recv[t, :1, :]
            ones = jnp.ones_like(own_total)
            own_factor, other_factor = jnp.exp(other_total), jnp.exp(own_total)
            own_is_far = first_core if way == 0 else jnp.logical_not(first_core)
            at = state_rows(way)
            s_send[t, at, :] = (
                jnp.where(own_is_far, own_factor, ones) * c_send[core, t, at, :]
                + jnp.where(own_is_far, ones, other_factor) * c_recv[t, at, :]
            )
            if way == 0:
                s_send[t, :8, :] = c_send[core, t, :8, :] + c_recv[t, :8, :]

            @pl.when(k < n_chip)
            def _():
                chip_out(way, k, t, chip).start()

            @pl.when(k == n_chip)
            def _():
                s_recv[t, rows_of(way)] = s_send[t, rows_of(way)]

        each_slice(one)

    give(0)
    each_slice(lambda k, t: own_part(0, core, t))
    give(1)
    join(0)
    each_slice(lambda k, t: own_part(1, core, t))
    join(1)

    b_rows, c_rows = projected[:, :state], projected[:, state:]
    scores = dot3(b_rows, c_rows, NT)
    for p in range(pairs):
        mixed = jnp.concatenate([grow[2 * p] * scores, grow[2 * p + 1] * scores], axis=1).astype(BF16)
        gx[:, p * 2 * size:(p + 1) * 2 * size] = dot(mixed, stacked(p))
    near_b = dot3(form, c_rows)
    near_c = dot3(jnp.transpose(form), b_rows)

    servers = n_out // 2

    def far_send(q, k, o):
        @pl.when(o // servers == q)
        def _():
            far_copy(S_FAR, k, o_send.at[o], o_recv.at[me_out], o).start()

    def far_step(forward):
        o_recv[me_out] = o_send[me_out]
        each_far(lambda k, o: far_copy(S_FAR, k, o_send.at[o], o_recv.at[lax.rem(me_out + n_out - k, n_out)], o).wait_recv())
        held = jnp.zeros((far, part), F32)
        for k in range(n_out):
            at = k if forward else n_out - 1 - k
            o_back[at] = held
            held = held * jnp.exp(o_recv[at, far:far + 1, :]) + o_recv[at, :far, :]
        each_far(lambda k, o: far_copy(S_BACK, k, o_back.at[o], carry.at[me_out], o).start())
        carry[me_out] = o_back[me_out]

    for way in range(WAYS):
        each_chip(lambda k, t: chip_out(way, k, t, lax.rem(chip + n_chip - k, n_chip)).wait_recv())
        if way == 0:
            totals = [s_recv[k, :1, :] for k in range(n_chip)]
            after, before = jnp.zeros((1, part), F32), jnp.zeros((1, part), F32)
            ahead, behind = [None] * n_chip, [None] * n_chip
            for k in range(n_chip):
                ahead[k], behind[n_chip - 1 - k] = jnp.exp(before), jnp.exp(after)
                before = before + totals[k]
                after = after + totals[n_chip - 1 - k]
            steps = [jnp.exp(t) for t in totals]
        held = jnp.zeros((state, part), F32)
        for k in range(n_chip - 1, -1, -1) if way else range(n_chip):
            prefix[k, state_rows(way, 0), :] = held
            held = held * steps[k] + s_recv[k, state_rows(way), :]
        for j in range(servers):
            o_send[way * servers + j, :far, :] = held[j * far:(j + 1) * far]
            o_send[way * servers + j, far:, :] = jnp.broadcast_to(before, (8, part))
        each_far(functools.partial(far_send, way))
    for forward in (True, False):
        pl.when((me_out < n_out // 2) == forward)(functools.partial(far_step, forward))

    def back_wait(q, k, o):
        source = lax.rem(me_out + n_out - k, n_out)

        @pl.when(source // servers == q)
        def _():
            far_copy(S_BACK, k, o_back.at[o], carry.at[source], o).wait_recv()

    def home_copy(way, k, t, source):
        at = state_rows(way, 0)
        return near_copy(S_HOME + way, k, s_back.at[t, at], s_home.at[source, at], t * 2 + core)

    for way in range(WAYS):
        each_far(functools.partial(back_wait, way))
        carried = jnp.concatenate([carry[way * servers + j] for j in range(servers)], axis=0)
        reach = behind if way else ahead
        at = state_rows(way, 0)
        for k in range(n_chip):
            s_back[k, at, :] = prefix[k, at, :] + reach[k] * carried
        each_chip(lambda k, t: home_copy(way, k, t, chip).start())
        s_home[chip, at, :] = s_back[chip, at, :]

    def core_home(way, k, side, t):
        at = state_rows(way, 0)
        return near_copy(C_HOME + way, k, c_back.at[t, at], states.at[side, t, at], chip * 2 + other)

    def use_part(way, side, t, sum_):
        at = lanes_of(side, t)
        values, rests = (xw_hi, xw_lo) if way else (gw_hi, gw_lo)
        got_hi, got_lo = split(states[side, t, state_rows(way, 0), :])
        both = dot(values[:, at], jnp.concatenate([got_hi, got_lo], axis=0), NT)
        return sum_ + both[:, :state] + both[:, state:] + dot(rests[:, at], got_hi, NT)

    def source_of(k):
        return lax.rem(chip + n_chip - k, n_chip)

    def share(way, k):
        t = source_of(k)
        at, tall = state_rows(way, 0), state_rows(way)
        got = s_home[t, at, :]
        by_own = jnp.exp(c_send[core, t, :1, :]) * got + c_send[core, t, tall, :]
        by_other = jnp.exp(c_recv[t, :1, :]) * got + c_recv[t, tall, :]
        comes_first = first_core if way == 0 else jnp.logical_not(first_core)
        states[core, t, at, :] = jnp.where(comes_first, got, by_other)
        c_back[t, at, :] = jnp.where(comes_first, by_own, got)
        core_home(way, k, core, t).start()

    sums = []
    for way, near in enumerate((near_c, near_b)):
        def share_arrived(k, sum_, way=way):
            t = source_of(k)
            home_copy(way, k, t, t).wait_recv()
            share(way, k)
            return use_part(way, core, t, sum_)

        def use_other(k, sum_, way=way):
            t = source_of(k)
            core_home(way, k, other, t).wait_recv()
            return use_part(way, other, t, sum_)

        share(way, 0)
        sum_ = use_part(way, core, chip, near)
        sum_ = lax.fori_loop(1, n_chip, share_arrived, sum_)
        sums.append(lax.fori_loop(0, n_chip, use_other, sum_))
    sums = sums[::-1]
    d_low = jnp.concatenate(sums, axis=1).astype(BF16)

    cut = width // n_out
    for o in range(n_out):
        g_send[o] = (dot(hidden_t[o * cut:(o + 1) * cut, :], d_low) * scale).astype(BF16)
    each_far(lambda k, o: far_copy(G_FAR, k, g_send.at[o], g_recv.at[me_out], o).start())
    g_recv[me_out] = g_send[me_out]

    gh[...] = dot(d_low, w, NT)
    store_gh = pltpu.make_async_copy(gh, gh_hbm, load_sem.at[0])
    store_gh.start()

    each_far(lambda k, o: far_copy(G_FAR, k, g_send.at[o], g_recv.at[lax.rem(me_out + n_out - k, n_out)], o).wait_recv())
    g_sum[...] = functools.reduce(lambda a, b: a + b, [g_recv[o].astype(F32) for o in range(n_out)])

    def owned(i):
        return g_sum.at[pl.ds(pl.multiple_of(i // per_tile * tile, tile), tile), :]

    each_near(lambda k, i: near_copy(G_NEAR, k, owned(i), g_near.at[me_in], i).start())
    g_near[me_in] = g_sum[pl.ds(pl.multiple_of(me_in // per_tile * tile, tile), tile), :]

    b_hi, b_lo = split(b_rows)
    b_three = jnp.concatenate([b_hi, b_lo, b_hi], axis=1)
    for i in range(n_in):
        at = slice(i * part, (i + 1) * part)
        got_hi, got_lo = split(states[i % 2, i // 2, state:, :])
        gx[:, at] = gx[:, at] + spread[:, at] * dot(b_three, jnp.concatenate([got_hi, got_hi, got_lo], axis=0))
    store_gx = pltpu.make_async_copy(gx, gx_hbm, load_sem.at[1])
    store_gx.start()

    each_near(lambda k, i: near_copy(G_NEAR, k, owned(i), g_near.at[lax.rem(me_in + n_in - k, n_in)], i).wait_recv())
    summed = functools.reduce(lambda a, b: a + b, [g_near[i] for i in range(n_in)])
    mine = summed[:own_rows]
    for q in range(1, per_tile):
        mine = jnp.where(lax.rem(me_in, per_tile) == q, summed[q * own_rows:(q + 1) * own_rows], mine)
    gp_ref[...] = mine

    each_near(lambda k, i: near_copy(W_NEAR, k, w_near.at[me_in], w_near.at[me_in], i).wait_send())
    each_far(lambda k, o: far_copy(W_FAR, k, w_far.at[me_out], w_far.at[me_out], o).wait_send())
    for way in range(WAYS):
        each_slice(lambda k, t: core_out(way, k, t).wait_send())
        each_chip(lambda k, t: chip_out(way, k, t, chip).wait_send())
        each_chip(lambda k, t: home_copy(way, k, t, chip).wait_send())
        each_slice(lambda k, t: core_home(way, k - 1, core, source_of(k - 1)).wait_send())
    each_far(lambda k, o: far_copy(S_FAR, k, o_send.at[o], o_recv.at[me_out], o).wait_send())
    each_far(lambda k, o: far_copy(S_BACK, k, o_back.at[o], carry.at[me_out], o).wait_send())
    each_far(lambda k, o: far_copy(G_FAR, k, g_send.at[o], g_recv.at[me_out], o).wait_send())
    each_near(lambda k, i: near_copy(G_NEAR, k, owned(i), g_near.at[me_in], i).wait_send())
    store_gh.wait()
    store_gx.wait()


def write_out(gx_from, gh_from, gp_from, gx_to, gh_to, gp_to, gx, gh, gp, sem):
    pieces = gx.shape[1]
    moves = [(gp_from, gp, gp_to)]
    for q in range(gx.shape[0]):
        at = slice(q * pieces, (q + 1) * pieces)
        moves.append((gx_from.at[at], gx.at[q], gx_to.at[at]))
        moves.append((gh_from.at[at], gh.at[q], gh_to.at[at]))
    reads = [pltpu.make_async_copy(m[0], m[1], sem.at[0, k]) for k, m in enumerate(moves)]
    writes = [pltpu.make_async_copy(m[1], m[2], sem.at[1, k]) for k, m in enumerate(moves)]
    for read in reads:
        read.start()
    for read, write in zip(reads, writes):
        read.wait()
        write.start()
    for write in writes:
        write.wait()


def per_device(hidden, x_act, dt_step, log_decay, w_bc, grad_y):
    n_out, n_in = lax.axis_size("outer"), lax.axis_size("inner")
    rows, width = hidden.shape
    lanes = x_act.shape[1]
    heads = dt_step.shape[1]
    own_rows, columns = w_bc.shape
    part = lanes // n_in
    far = columns // n_out
    tile = max(8, own_rows)
    most = max(n_out, n_in)
    scale = 1.0 / math.sqrt(rows * n_out * n_in)
    anywhere = pl.BlockSpec(memory_space=pl.ANY)
    vmem = pl.BlockSpec(memory_space=pltpu.VMEM)
    results = pl.pallas_call(
        functools.partial(kernel, scale, n_out, n_in),
        out_shape=(
            jax.ShapeDtypeStruct((rows, lanes), F32),
            jax.ShapeDtypeStruct((rows, width), F32),
            jax.ShapeDtypeStruct((own_rows, columns), F32),
        ),
        in_specs=[anywhere, anywhere, anywhere, anywhere, vmem, anywhere],
        out_specs=(anywhere, anywhere, vmem),
        scratch_shapes=[
            pltpu.VMEM((rows, width), BF16),
            pltpu.VMEM((rows, lanes), BF16),
            pltpu.VMEM((rows, lanes), BF16),
            pltpu.VMEM((heads, rows), F32),
            pltpu.VMEM((heads, rows), F32),
            pltpu.VMEM((width, rows), BF16),
            pltpu.VMEM((rows, lanes), F32),
            pltpu.VMEM((rows, width), F32),
            pltpu.VMEM((n_in, tile, columns), F32),
            pltpu.VMEM((n_out, width // n_out, columns), BF16),
            pltpu.VMEM((heads, rows, rows), F32),
            pltpu.VMEM((rows, lanes), F32),
            pltpu.VMEM((rows, lanes), BF16),
            pltpu.VMEM((rows, lanes), BF16),
            pltpu.VMEM((rows, lanes), BF16),
            pltpu.VMEM((rows, lanes), BF16),
            pltpu.VMEM((2, n_in // 2, columns + 8, part), F32),
            pltpu.VMEM((n_in // 2, columns + 8, part), F32),
            pltpu.VMEM((n_in // 2, columns + 8, part), F32),
            pltpu.VMEM((n_in // 2, columns + 8, part), F32),
            pltpu.VMEM((n_in // 2, columns, part), F32),
            pltpu.VMEM((n_out, far + 8, part), F32),
            pltpu.VMEM((n_out, far + 8, part), F32),
            pltpu.VMEM((n_out, far, part), F32),
            pltpu.VMEM((n_out, far, part), F32),
            pltpu.VMEM((n_in // 2, columns, part), F32),
            pltpu.VMEM((n_in // 2, columns, part), F32),
            pltpu.VMEM((n_in // 2, columns, part), F32),
            pltpu.VMEM((2, n_in // 2, columns, part), F32),
            pltpu.VMEM((n_out, width // n_out, columns), BF16),
            pltpu.VMEM((n_out, width // n_out, columns), BF16),
            pltpu.VMEM((width // n_out, columns), F32),
            pltpu.VMEM((n_in, tile, columns), F32),
            pltpu.SemaphoreType.DMA((5,)),
            pltpu.SemaphoreType.DMA((PHASES, most)),
            pltpu.SemaphoreType.DMA((PHASES, most)),
        ],
        compiler_params=pltpu.CompilerParams(
            collective_id=0, has_side_effects=True, vmem_limit_bytes=60 * 1024 * 1024
        ),
        cost_estimate=pl.CostEstimate(flops=10**9, bytes_accessed=3 * 10**6, transcendentals=10**6),
    )(hidden, x_act, dt_step.T, log_decay.T, w_bc, grad_y)
    pieces = rows // 4
    return pl.pallas_call(
        write_out,
        out_shape=tuple(jax.ShapeDtypeStruct(r.shape, r.dtype) for r in results),
        in_specs=[anywhere] * 3,
        out_specs=(anywhere,) * 3,
        scratch_shapes=[
            pltpu.VMEM((4, pieces, lanes), F32),
            pltpu.VMEM((4, pieces, width), F32),
            pltpu.VMEM((own_rows, columns), F32),
            pltpu.SemaphoreType.DMA((2, 9)),
        ],
        compiler_params=pltpu.CompilerParams(vmem_limit_bytes=60 * 1024 * 1024),
    )(*results)


def solution(mesh):
    spec = P(("outer", "inner"), None)
    return jax.shard_map(
        per_device, mesh=mesh, in_specs=(spec,) * 6, out_specs=(spec,) * 3, check_vma=False
    )
```

```python
import functools
import math

import jax
import jax.numpy as jnp
from jax import lax
from jax.experimental import pallas as pl
from jax.experimental.pallas import tpu as pltpu
from jax.sharding import PartitionSpec as P

BF16 = jnp.bfloat16
F32 = jnp.float32
MESH = pl.DeviceIdType.MESH
HIGH = lax.Precision.HIGHEST

NN = (((1,), (0,)), ((), ()))
NT = (((1,), (1,)), ((), ()))

W_NEAR, W_FAR, S_FAR, S_BACK, G_FAR, G_NEAR, S_OUT = range(7)
WAYS = 2
S_HOME = S_OUT + WAYS
C_OUT = S_HOME + WAYS
C_HOME = C_OUT + WAYS
PHASES = C_HOME + WAYS


def dot(a, b, dims=NN):
    return lax.dot_general(a, b, dims, preferred_element_type=F32)


def split(value):
    high = value.astype(BF16)
    return high, (value - high.astype(F32)).astype(BF16)


def dot3(a, b, dims=NN):
    a_high, a_low = split(a)
    b_high, b_low = split(b)
    return dot(a_high, b_high, dims) + dot(a_high, b_low, dims) + dot(a_low, b_high, dims)


def iota(shape, axis):
    return lax.broadcasted_iota(jnp.int32, shape, axis)


def kernel(
    scale, n_out, n_in,
    hidden_hbm, x_hbm, dt_hbm, decay_hbm, w_ref, gy_hbm,
    gx_hbm, gh_hbm, gp_ref,
    hidden, x, gy, dt_ref, decay_ref, hidden_t, gx, gh,
    w_near, w_far, grow, spread, xw_hi, xw_lo, gw_hi, gw_lo,
    c_send, c_recv, s_send, s_recv, prefix, o_send, o_recv, o_back, carry, s_back, s_home, c_back, states,
    g_send, g_recv, g_sum, g_near,
    load_sem, send_sem, recv_sem,
):
    me_out, me_in = lax.axis_index("outer"), lax.axis_index("inner")
    rows, width = hidden.shape
    lanes = x.shape[1]
    heads = dt_ref.shape[0]
    size = lanes // heads
    state = w_far.shape[2] // 2
    part = lanes // n_in
    far = 2 * state // n_out
    pairs = heads // 2
    n_chip = n_in // 2
    chip, core = me_in // 2, lax.rem(me_in, 2)
    other = 1 - core

    loads = [
        pltpu.make_async_copy(source, target, load_sem.at[k])
        for k, (source, target) in enumerate(
            ((decay_hbm, decay_ref), (dt_hbm, dt_ref), (x_hbm, x), (gy_hbm, gy), (hidden_hbm, hidden))
        )
    ]
    for load in loads:
        load.start()

    barrier = pltpu.get_barrier_semaphore()

    def each_near(act):
        lax.fori_loop(1, n_in, lambda k, c: (act(k, lax.rem(me_in + k, n_in)), c)[1], 0)

    def each_chip(act):
        lax.fori_loop(1, n_chip, lambda k, c: (act(k, lax.rem(chip + k, n_chip)), c)[1], 0)

    def each_far(act):
        lax.fori_loop(1, n_out, lambda k, c: (act(k, lax.rem(me_out + k, n_out)), c)[1], 0)

    def greet(*place):
        pl.semaphore_signal(barrier, inc=1, device_id=place, device_id_type=MESH)

    each_near(lambda k, i: greet(me_out, i))
    each_far(lambda k, o: greet(o, me_in))

    def near_copy(phase, k, source, target, i):
        return pltpu.make_async_remote_copy(
            src_ref=source, dst_ref=target, send_sem=send_sem.at[phase, k], recv_sem=recv_sem.at[phase, k],
            device_id=(me_out, i), device_id_type=MESH,
        )

    def far_copy(phase, k, source, target, o):
        return pltpu.make_async_remote_copy(
            src_ref=source, dst_ref=target, send_sem=send_sem.at[phase, k], recv_sem=recv_sem.at[phase, k],
            device_id=(o, me_in), device_id_type=MESH,
        )

    own_rows = w_ref.shape[0]
    tile = w_near.shape[1]
    per_tile = tile // own_rows
    own_w = jnp.concatenate([w_ref[...].astype(F32)] * per_tile, axis=0)
    own_w = jnp.where(iota(own_w.shape, 0) // own_rows == lax.rem(me_in, per_tile), own_w, 0.0)
    w_near[me_in] = own_w

    pl.semaphore_wait(barrier, n_in + n_out - 2)
    each_near(lambda k, i: near_copy(W_NEAR, k, w_near.at[me_in], w_near.at[me_in], i).start())

    loads[0].wait()
    loads[1].wait()
    upto = (iota((rows, rows), 0) <= iota((rows, rows), 1)).astype(F32)
    running_t = lax.dot_general(decay_ref[...], upto, NN, precision=HIGH, preferred_element_type=F32)
    dt_t = dt_ref[...]
    total_t = jnp.broadcast_to(running_t[:, rows - 1:], running_t.shape)
    columns = jnp.transpose(jnp.concatenate(
        [dt_t * jnp.exp(total_t - running_t), jnp.exp(running_t), total_t, running_t - jnp.log(dt_t)], axis=0
    ))
    shifted = columns[:, 3 * heads:]
    stack = jnp.concatenate(
        [columns[:, :heads], columns[:, heads:2 * heads], columns[:8, 2 * heads:3 * heads]], axis=0
    )
    high = stack.astype(BF16)
    rest = stack - high.astype(F32)
    middle = rest.astype(BF16)
    low = (rest - middle.astype(F32)).astype(BF16)
    stack = jnp.concatenate([high, middle, low], axis=1)
    for load in loads[2:]:
        load.wait()
    for c in range(lanes // 256):
        at = slice(c * 256, (c + 1) * 256)
        chosen = lax.rem(iota((3 * heads, 256), 0), heads) == (iota((3 * heads, 256), 1) + c * 256) // size
        wide = dot(stack, jnp.where(chosen, 1.0, 0.0).astype(BF16))
        spread[:, at] = wide[:rows]
        xw_hi[:, at], xw_lo[:, at] = split(x[:, at].astype(F32) * wide[:rows])
        gw_hi[:, at], gw_lo[:, at] = split(gy[:, at].astype(F32) * wide[rows:2 * rows])
        for q in range(max(1, 256 // part)):
            lane = c * 256 + q * part
            cut = min(part, 256)
            i = lane // part
            c_send[i % 2, i // 2, :8, lane % part:lane % part + cut] = wide[2 * rows:, q * part:q * part + cut]

    each_near(lambda k, i: near_copy(W_NEAR, k, w_near.at[me_in], w_near.at[lax.rem(me_in + n_in - k, n_in)], i).wait_recv())
    block = [
        functools.reduce(lambda a, b: a + b, [w_near[t * per_tile + q] for q in range(per_tile)])
        for t in range(n_in // per_tile)
    ]
    w_far[me_out] = jnp.concatenate(block, axis=0).astype(BF16)
    each_far(lambda k, o: far_copy(W_FAR, k, w_far.at[me_out], w_far.at[me_out], o).start())

    left = iota((rows, 2 * size), 1) < size
    keep = iota((rows, rows), 0) <= iota((rows, rows), 1)
    form = jnp.zeros((rows, rows), F32)

    def stacked(p):
        g = gy[:, p * 2 * size:(p + 1) * 2 * size]
        zero = jnp.zeros_like(g)
        return jnp.concatenate([jnp.where(left, g, zero), jnp.where(left, zero, g)], axis=0)

    for p in range(pairs):
        products = dot(x[:, p * 2 * size:(p + 1) * 2 * size], stacked(p), NT)
        for q in range(2):
            h = 2 * p + q
            spans = running_t[h:h + 1, :] - shifted[:, h:h + 1]
            factor = jnp.exp(jnp.where(keep, spans, -1e30))
            grow[h] = factor
            form = form + factor * products[:, q * rows:(q + 1) * rows]
    for c in range(width // 128):
        hidden_t[c * 128:(c + 1) * 128, :] = jnp.transpose(hidden[:, c * 128:(c + 1) * 128])

    each_far(lambda k, o: far_copy(W_FAR, k, w_far.at[me_out], w_far.at[lax.rem(me_out + n_out - k, n_out)], o).wait_recv())
    w = w_far[...].reshape(width, 2 * state)
    projected = dot(hidden[...], w)
    projected_t = jnp.transpose(projected)
    proj_hi, proj_lo = split(projected_t)
    b_t = jnp.concatenate([proj_hi[:state], proj_lo[:state]], axis=0)
    c_t = jnp.concatenate([proj_hi[state:], proj_lo[state:]], axis=0)

    def rows_of(way):
        return slice(8 + state, 8 + 2 * state) if way else slice(0, 8 + state)

    def state_rows(way, first=8):
        return slice(first + way * state, first + (way + 1) * state)

    def lanes_of(side, t):
        return pl.ds(pl.multiple_of((t * 2 + side) * part, part), part)

    def side_lanes(ref, side):
        return jnp.concatenate([ref[:, lanes_of(side, t)] for t in range(n_chip)], axis=1)

    def own_half(way, side):
        which = c_t if way else b_t
        values, rests = (gw_hi, gw_lo) if way else (xw_hi, xw_lo)
        both = dot(which, side_lanes(values, side))
        made = both[:state] + both[state:] + dot(which[:state], side_lanes(rests, side))
        for t in range(n_chip):
            c_send[side, t, state_rows(way), :] = made[:, t * part:(t + 1) * part]

    def core_out(way, k, t):
        return near_copy(C_OUT + way, k, c_send.at[other, t, rows_of(way)], c_recv.at[t, rows_of(way)], chip * 2 + other)

    def chip_out(way, k, t, source):
        return near_copy(S_OUT + way, k, s_send.at[t, rows_of(way)], s_recv.at[source, rows_of(way)], t * 2 + core)

    def each_slice(act):
        lax.fori_loop(1, n_chip + 1, lambda k, c: (act(k, lax.rem(chip + k, n_chip)), c)[1], 0)

    def give(way):
        own_half(way, other)
        each_slice(lambda k, t: core_out(way, k, t).start())

    first_core = core == 0

    def join(way):
        def one(k, t):
            core_out(way, k, t).wait_recv()
            own_total, other_total = c_send[core, t, :1, :], c_recv[t, :1, :]
            ones = jnp.ones_like(own_total)
            own_factor, other_factor = jnp.exp(other_total), jnp.exp(own_total)
            own_is_far = first_core if way == 0 else jnp.logical_not(first_core)
            at = state_rows(way)
            s_send[t, at, :] = (
                jnp.where(own_is_far, own_factor, ones) * c_send[core, t, at, :]
                + jnp.where(own_is_far, ones, other_factor) * c_recv[t, at, :]
            )
            if way == 0:
                s_send[t, :8, :] = c_send[core, t, :8, :] + c_recv[t, :8, :]

            @pl.when(k < n_chip)
            def _():
                chip_out(way, k, t, chip).start()

            @pl.when(k == n_chip)
            def _():
                s_recv[t, rows_of(way)] = s_send[t, rows_of(way)]

        each_slice(one)

    give(0)
    own_half(0, core)
    give(1)
    join(0)
    own_half(1, core)
    join(1)

    b_rows, c_rows = projected[:, :state], projected[:, state:]
    scores = dot3(b_rows, c_rows, NT)
    for p in range(pairs):
        mixed = jnp.concatenate([grow[2 * p] * scores, grow[2 * p + 1] * scores], axis=1).astype(BF16)
        gx[:, p * 2 * size:(p + 1) * 2 * size] = dot(mixed, stacked(p))
    near_b = dot3(form, c_rows)
    near_c = dot3(jnp.transpose(form), b_rows)

    servers = n_out // 2

    def far_send(q, k, o):
        @pl.when(o // servers == q)
        def _():
            far_copy(S_FAR, k, o_send.at[o], o_recv.at[me_out], o).start()

    def far_step(forward):
        o_recv[me_out] = o_send[me_out]
        each_far(lambda k, o: far_copy(S_FAR, k, o_send.at[o], o_recv.at[lax.rem(me_out + n_out - k, n_out)], o).wait_recv())
        held = jnp.zeros((far, part), F32)
        for k in range(n_out):
            at = k if forward else n_out - 1 - k
            o_back[at] = held
            held = held * jnp.exp(o_recv[at, far:far + 1, :]) + o_recv[at, :far, :]
        each_far(lambda k, o: far_copy(S_BACK, k, o_back.at[o], carry.at[me_out], o).start())
        carry[me_out] = o_back[me_out]

    for way in range(WAYS):
        each_chip(lambda k, t: chip_out(way, k, t, lax.rem(chip + n_chip - k, n_chip)).wait_recv())
        if way == 0:
            totals = [s_recv[k, :1, :] for k in range(n_chip)]
            after, before = jnp.zeros((1, part), F32), jnp.zeros((1, part), F32)
            ahead, behind = [None] * n_chip, [None] * n_chip
            for k in range(n_chip):
                ahead[k], behind[n_chip - 1 - k] = jnp.exp(before), jnp.exp(after)
                before = before + totals[k]
                after = after + totals[n_chip - 1 - k]
            steps = [jnp.exp(t) for t in totals]
        held = jnp.zeros((state, part), F32)
        for k in range(n_chip - 1, -1, -1) if way else range(n_chip):
            prefix[k, state_rows(way, 0), :] = held
            held = held * steps[k] + s_recv[k, state_rows(way), :]
        for j in range(servers):
            o_send[way * servers + j, :far, :] = held[j * far:(j + 1) * far]
            o_send[way * servers + j, far:, :] = jnp.broadcast_to(before, (8, part))
        each_far(functools.partial(far_send, way))
    for forward in (True, False):
        pl.when((me_out < n_out // 2) == forward)(functools.partial(far_step, forward))

    def back_wait(q, k, o):
        source = lax.rem(me_out + n_out - k, n_out)

        @pl.when(source // servers == q)
        def _():
            far_copy(S_BACK, k, o_back.at[o], carry.at[source], o).wait_recv()

    def home_copy(way, k, t, source):
        at = state_rows(way, 0)
        return near_copy(S_HOME + way, k, s_back.at[t, at], s_home.at[source, at], t * 2 + core)

    for way in range(WAYS):
        each_far(functools.partial(back_wait, way))
        carried = jnp.concatenate([carry[way * servers + j] for j in range(servers)], axis=0)
        reach = behind if way else ahead
        at = state_rows(way, 0)
        for k in range(n_chip):
            s_back[k, at, :] = prefix[k, at, :] + reach[k] * carried
        each_chip(lambda k, t: home_copy(way, k, t, chip).start())
        s_home[chip, at, :] = s_back[chip, at, :]

    def core_home(way, k, side, t):
        at = state_rows(way, 0)
        return near_copy(C_HOME + way, k, c_back.at[t, at], states.at[side, t, at], chip * 2 + other)

    def use_half(way, side, sum_):
        values, rests = (xw_hi, xw_lo) if way else (gw_hi, gw_lo)
        got = jnp.concatenate([states[side, t, state_rows(way, 0), :] for t in range(n_chip)], axis=1)
        got_hi, got_lo = split(got)
        both = dot(side_lanes(values, side), jnp.concatenate([got_hi, got_lo], axis=0), NT)
        return sum_ + both[:, :state] + both[:, state:] + dot(side_lanes(rests, side), got_hi, NT)

    def source_of(k):
        return lax.rem(chip + n_chip - k, n_chip)

    def share(way, k):
        t = source_of(k)
        at, tall = state_rows(way, 0), state_rows(way)
        got = s_home[t, at, :]
        by_own = jnp.exp(c_send[core, t, :1, :]) * got + c_send[core, t, tall, :]
        by_other = jnp.exp(c_recv[t, :1, :]) * got + c_recv[t, tall, :]
        comes_first = first_core if way == 0 else jnp.logical_not(first_core)
        states[core, t, at, :] = jnp.where(comes_first, got, by_other)
        c_back[t, at, :] = jnp.where(comes_first, by_own, got)
        core_home(way, k, core, t).start()

    sums = []
    for way, near in enumerate((near_c, near_b)):
        def share_arrived(k, t):
            source = source_of(k)
            home_copy(way, k, source, source).wait_recv()
            share(way, k)

        share(way, 0)
        each_chip(share_arrived)
        sum_ = use_half(way, core, near)
        each_slice(lambda k, t: core_home(way, k - 1, other, source_of(k - 1)).wait_recv())
        sums.append(use_half(way, other, sum_))
    sums = sums[::-1]
    d_low = jnp.concatenate(sums, axis=1).astype(BF16)

    cut = width // n_out
    for q in range(2):
        term = (dot(hidden_t[q * width // 2:(q + 1) * width // 2, :], d_low) * scale).astype(BF16)
        for o in range(n_out // 2):
            g_send[q * n_out // 2 + o] = term[o * cut:(o + 1) * cut]
    each_far(lambda k, o: far_copy(G_FAR, k, g_send.at[o], g_recv.at[me_out], o).start())
    g_recv[me_out] = g_send[me_out]

    gh[...] = dot(d_low, w, NT)
    store_gh = pltpu.make_async_copy(gh, gh_hbm, load_sem.at[0])
    store_gh.start()

    each_far(lambda k, o: far_copy(G_FAR, k, g_send.at[o], g_recv.at[lax.rem(me_out + n_out - k, n_out)], o).wait_recv())
    g_sum[...] = functools.reduce(lambda a, b: a + b, [g_recv[o].astype(F32) for o in range(n_out)])

    def owned(i):
        return g_sum.at[pl.ds(pl.multiple_of(i // per_tile * tile, tile), tile), :]

    each_near(lambda k, i: near_copy(G_NEAR, k, owned(i), g_near.at[me_in], i).start())
    g_near[me_in] = g_sum[pl.ds(pl.multiple_of(me_in // per_tile * tile, tile), tile), :]

    b_hi, b_lo = split(b_rows)
    b_three = jnp.concatenate([b_hi, b_lo, b_hi], axis=1)
    for i in range(n_in):
        at = slice(i * part, (i + 1) * part)
        got_hi, got_lo = split(states[i % 2, i // 2, state:, :])
        gx[:, at] = gx[:, at] + spread[:, at] * dot(b_three, jnp.concatenate([got_hi, got_hi, got_lo], axis=0))
    store_gx = pltpu.make_async_copy(gx, gx_hbm, load_sem.at[1])
    store_gx.start()

    each_near(lambda k, i: near_copy(G_NEAR, k, owned(i), g_near.at[lax.rem(me_in + n_in - k, n_in)], i).wait_recv())
    summed = functools.reduce(lambda a, b: a + b, [g_near[i] for i in range(n_in)])
    mine = summed[:own_rows]
    for q in range(1, per_tile):
        mine = jnp.where(lax.rem(me_in, per_tile) == q, summed[q * own_rows:(q + 1) * own_rows], mine)
    gp_ref[...] = mine

    each_near(lambda k, i: near_copy(W_NEAR, k, w_near.at[me_in], w_near.at[me_in], i).wait_send())
    each_far(lambda k, o: far_copy(W_FAR, k, w_far.at[me_out], w_far.at[me_out], o).wait_send())
    for way in range(WAYS):
        each_slice(lambda k, t: core_out(way, k, t).wait_send())
        each_chip(lambda k, t: chip_out(way, k, t, chip).wait_send())
        each_chip(lambda k, t: home_copy(way, k, t, chip).wait_send())
        each_slice(lambda k, t: core_home(way, k - 1, core, source_of(k - 1)).wait_send())
    each_far(lambda k, o: far_copy(S_FAR, k, o_send.at[o], o_recv.at[me_out], o).wait_send())
    each_far(lambda k, o: far_copy(S_BACK, k, o_back.at[o], carry.at[me_out], o).wait_send())
    each_far(lambda k, o: far_copy(G_FAR, k, g_send.at[o], g_recv.at[me_out], o).wait_send())
    each_near(lambda k, i: near_copy(G_NEAR, k, owned(i), g_near.at[me_in], i).wait_send())
    store_gh.wait()
    store_gx.wait()


def write_out(gx_from, gh_from, gp_from, gx_to, gh_to, gp_to, gx, gh, gp, sem):
    pieces = gx.shape[1]
    moves = [(gp_from, gp, gp_to)]
    for q in range(gx.shape[0]):
        at = slice(q * pieces, (q + 1) * pieces)
        moves.append((gx_from.at[at], gx.at[q], gx_to.at[at]))
        moves.append((gh_from.at[at], gh.at[q], gh_to.at[at]))
    reads = [pltpu.make_async_copy(m[0], m[1], sem.at[0, k]) for k, m in enumerate(moves)]
    writes = [pltpu.make_async_copy(m[1], m[2], sem.at[1, k]) for k, m in enumerate(moves)]
    for read in reads:
        read.start()
    for read, write in zip(reads, writes):
        read.wait()
        write.start()
    for write in writes:
        write.wait()


def per_device(hidden, x_act, dt_step, log_decay, w_bc, grad_y):
    n_out, n_in = lax.axis_size("outer"), lax.axis_size("inner")
    rows, width = hidden.shape
    lanes = x_act.shape[1]
    heads = dt_step.shape[1]
    own_rows, columns = w_bc.shape
    part = lanes // n_in
    far = columns // n_out
    tile = max(8, own_rows)
    most = max(n_out, n_in)
    scale = 1.0 / math.sqrt(rows * n_out * n_in)
    anywhere = pl.BlockSpec(memory_space=pl.ANY)
    vmem = pl.BlockSpec(memory_space=pltpu.VMEM)
    results = pl.pallas_call(
        functools.partial(kernel, scale, n_out, n_in),
        out_shape=(
            jax.ShapeDtypeStruct((rows, lanes), F32),
            jax.ShapeDtypeStruct((rows, width), F32),
            jax.ShapeDtypeStruct((own_rows, columns), F32),
        ),
        in_specs=[anywhere, anywhere, anywhere, anywhere, vmem, anywhere],
        out_specs=(anywhere, anywhere, vmem),
        scratch_shapes=[
            pltpu.VMEM((rows, width), BF16),
            pltpu.VMEM((rows, lanes), BF16),
            pltpu.VMEM((rows, lanes), BF16),
            pltpu.VMEM((heads, rows), F32),
            pltpu.VMEM((heads, rows), F32),
            pltpu.VMEM((width, rows), BF16),
            pltpu.VMEM((rows, lanes), F32),
            pltpu.VMEM((rows, width), F32),
            pltpu.VMEM((n_in, tile, columns), F32),
            pltpu.VMEM((n_out, width // n_out, columns), BF16),
            pltpu.VMEM((heads, rows, rows), F32),
            pltpu.VMEM((rows, lanes), F32),
            pltpu.VMEM((rows, lanes), BF16),
            pltpu.VMEM((rows, lanes), BF16),
            pltpu.VMEM((rows, lanes), BF16),
            pltpu.VMEM((rows, lanes), BF16),
            pltpu.VMEM((2, n_in // 2, columns + 8, part), F32),
            pltpu.VMEM((n_in // 2, columns + 8, part), F32),
            pltpu.VMEM((n_in // 2, columns + 8, part), F32),
            pltpu.VMEM((n_in // 2, columns + 8, part), F32),
            pltpu.VMEM((n_in // 2, columns, part), F32),
            pltpu.VMEM((n_out, far + 8, part), F32),
            pltpu.VMEM((n_out, far + 8, part), F32),
            pltpu.VMEM((n_out, far, part), F32),
            pltpu.VMEM((n_out, far, part), F32),
            pltpu.VMEM((n_in // 2, columns, part), F32),
            pltpu.VMEM((n_in // 2, columns, part), F32),
            pltpu.VMEM((n_in // 2, columns, part), F32),
            pltpu.VMEM((2, n_in // 2, columns, part), F32),
            pltpu.VMEM((n_out, width // n_out, columns), BF16),
            pltpu.VMEM((n_out, width // n_out, columns), BF16),
            pltpu.VMEM((width // n_out, columns), F32),
            pltpu.VMEM((n_in, tile, columns), F32),
            pltpu.SemaphoreType.DMA((5,)),
            pltpu.SemaphoreType.DMA((PHASES, most)),
            pltpu.SemaphoreType.DMA((PHASES, most)),
        ],
        compiler_params=pltpu.CompilerParams(
            collective_id=0, has_side_effects=True, vmem_limit_bytes=60 * 1024 * 1024
        ),
        cost_estimate=pl.CostEstimate(flops=10**9, bytes_accessed=3 * 10**6, transcendentals=10**6),
    )(hidden, x_act, dt_step.T, log_decay.T, w_bc, grad_y)
    pieces = rows // 4
    return pl.pallas_call(
        write_out,
        out_shape=tuple(jax.ShapeDtypeStruct(r.shape, r.dtype) for r in results),
        in_specs=[anywhere] * 3,
        out_specs=(anywhere,) * 3,
        scratch_shapes=[
            pltpu.VMEM((4, pieces, lanes), F32),
            pltpu.VMEM((4, pieces, width), F32),
            pltpu.VMEM((own_rows, columns), F32),
            pltpu.SemaphoreType.DMA((2, 9)),
        ],
        compiler_params=pltpu.CompilerParams(vmem_limit_bytes=60 * 1024 * 1024),
    )(*results)


def solution(mesh):
    spec = P(("outer", "inner"), None)
    return jax.shard_map(
        per_device, mesh=mesh, in_specs=(spec,) * 6, out_specs=(spec,) * 3, check_vma=False
    )
```

```python
import functools
import math

import jax
import jax.numpy as jnp
from jax import lax
from jax.experimental import pallas as pl
from jax.experimental.pallas import tpu as pltpu
from jax.sharding import PartitionSpec as P

BF16 = jnp.bfloat16
F32 = jnp.float32
MESH = pl.DeviceIdType.MESH
HIGH = lax.Precision.HIGHEST

NN = (((1,), (0,)), ((), ()))
NT = (((1,), (1,)), ((), ()))

W_NEAR, W_FAR, S_FAR, S_BACK, G_NEAR, S_OUT = range(6)
WAYS = 2
S_HOME = S_OUT + WAYS
C_OUT = S_HOME + WAYS
C_HOME = C_OUT + WAYS
G_FAR = C_HOME + WAYS
PHASES = G_FAR + WAYS


def dot(a, b, dims=NN):
    return lax.dot_general(a, b, dims, preferred_element_type=F32)


def split(value):
    high = value.astype(BF16)
    return high, (value - high.astype(F32)).astype(BF16)


def dot3(a, b, dims=NN):
    a_high, a_low = split(a)
    b_high, b_low = split(b)
    return dot(a_high, b_high, dims) + dot(a_high, b_low, dims) + dot(a_low, b_high, dims)


def iota(shape, axis):
    return lax.broadcasted_iota(jnp.int32, shape, axis)


def kernel(
    scale, n_out, n_in,
    hidden_hbm, x_hbm, dt_hbm, decay_hbm, w_ref, gy_hbm,
    gx_hbm, gh_hbm, gp_ref,
    hidden, x, gy, dt_ref, decay_ref, hidden_t, gx, gh,
    w_near, w_far, grow, spread, xw_hi, xw_lo, gw_hi, gw_lo,
    c_send, c_recv, s_send, s_recv, prefix, o_send, o_recv, o_back, carry, s_back, s_home, c_back, states,
    g_send, g_recv, g_sum, g_near,
    load_sem, send_sem, recv_sem,
):
    me_out, me_in = lax.axis_index("outer"), lax.axis_index("inner")
    rows, width = hidden.shape
    lanes = x.shape[1]
    heads = dt_ref.shape[0]
    size = lanes // heads
    state = w_far.shape[2] // 2
    part = lanes // n_in
    far = 2 * state // n_out
    pairs = heads // 2
    n_chip = n_in // 2
    chip, core = me_in // 2, lax.rem(me_in, 2)
    other = 1 - core

    loads = [
        pltpu.make_async_copy(source, target, load_sem.at[k])
        for k, (source, target) in enumerate(
            ((decay_hbm, decay_ref), (dt_hbm, dt_ref), (x_hbm, x), (gy_hbm, gy), (hidden_hbm, hidden))
        )
    ]
    for load in loads:
        load.start()

    barrier = pltpu.get_barrier_semaphore()

    def each_near(act):
        lax.fori_loop(1, n_in, lambda k, c: (act(k, lax.rem(me_in + k, n_in)), c)[1], 0)

    def each_chip(act):
        lax.fori_loop(1, n_chip, lambda k, c: (act(k, lax.rem(chip + k, n_chip)), c)[1], 0)

    def each_far(act):
        lax.fori_loop(1, n_out, lambda k, c: (act(k, lax.rem(me_out + k, n_out)), c)[1], 0)

    def greet(*place):
        pl.semaphore_signal(barrier, inc=1, device_id=place, device_id_type=MESH)

    each_near(lambda k, i: greet(me_out, i))
    each_far(lambda k, o: greet(o, me_in))

    def near_copy(phase, k, source, target, i):
        return pltpu.make_async_remote_copy(
            src_ref=source, dst_ref=target, send_sem=send_sem.at[phase, k], recv_sem=recv_sem.at[phase, k],
            device_id=(me_out, i), device_id_type=MESH,
        )

    def far_copy(phase, k, source, target, o):
        return pltpu.make_async_remote_copy(
            src_ref=source, dst_ref=target, send_sem=send_sem.at[phase, k], recv_sem=recv_sem.at[phase, k],
            device_id=(o, me_in), device_id_type=MESH,
        )

    own_rows = w_ref.shape[0]
    tile = w_near.shape[1]
    per_tile = tile // own_rows
    own_w = jnp.concatenate([w_ref[...].astype(F32)] * per_tile, axis=0)
    own_w = jnp.where(iota(own_w.shape, 0) // own_rows == lax.rem(me_in, per_tile), own_w, 0.0)
    w_near[me_in] = own_w

    pl.semaphore_wait(barrier, n_in + n_out - 2)
    each_near(lambda k, i: near_copy(W_NEAR, k, w_near.at[me_in], w_near.at[me_in], i).start())

    loads[0].wait()
    loads[1].wait()
    upto = (iota((rows, rows), 0) <= iota((rows, rows), 1)).astype(F32)
    running_t = lax.dot_general(decay_ref[...], upto, NN, precision=HIGH, preferred_element_type=F32)
    dt_t = dt_ref[...]
    total_t = jnp.broadcast_to(running_t[:, rows - 1:], running_t.shape)
    columns = jnp.transpose(jnp.concatenate(
        [dt_t * jnp.exp(total_t - running_t), jnp.exp(running_t), total_t, running_t - jnp.log(dt_t)], axis=0
    ))
    shifted = columns[:, 3 * heads:]
    stack = jnp.concatenate(
        [columns[:, :heads], columns[:, heads:2 * heads], columns[:8, 2 * heads:3 * heads]], axis=0
    )
    high = stack.astype(BF16)
    rest = stack - high.astype(F32)
    middle = rest.astype(BF16)
    low = (rest - middle.astype(F32)).astype(BF16)
    stack = jnp.concatenate([high, middle, low], axis=1)
    for load in loads[2:]:
        load.wait()
    for c in range(lanes // 256):
        at = slice(c * 256, (c + 1) * 256)
        chosen = lax.rem(iota((3 * heads, 256), 0), heads) == (iota((3 * heads, 256), 1) + c * 256) // size
        wide = dot(stack, jnp.where(chosen, 1.0, 0.0).astype(BF16))
        spread[:, at] = wide[:rows]
        xw_hi[:, at], xw_lo[:, at] = split(x[:, at].astype(F32) * wide[:rows])
        gw_hi[:, at], gw_lo[:, at] = split(gy[:, at].astype(F32) * wide[rows:2 * rows])
        for q in range(max(1, 256 // part)):
            lane = c * 256 + q * part
            cut = min(part, 256)
            i = lane // part
            c_send[i % 2, i // 2, :8, lane % part:lane % part + cut] = wide[2 * rows:, q * part:q * part + cut]

    each_near(lambda k, i: near_copy(W_NEAR, k, w_near.at[me_in], w_near.at[lax.rem(me_in + n_in - k, n_in)], i).wait_recv())
    block = [
        functools.reduce(lambda a, b: a + b, [w_near[t * per_tile + q] for q in range(per_tile)])
        for t in range(n_in // per_tile)
    ]
    w_far[me_out] = jnp.concatenate(block, axis=0).astype(BF16)
    each_far(lambda k, o: far_copy(W_FAR, k, w_far.at[me_out], w_far.at[me_out], o).start())

    left = iota((rows, 2 * size), 1) < size
    keep = iota((rows, rows), 0) <= iota((rows, rows), 1)
    form = jnp.zeros((rows, rows), F32)

    def stacked(p):
        g = gy[:, p * 2 * size:(p + 1) * 2 * size]
        zero = jnp.zeros_like(g)
        return jnp.concatenate([jnp.where(left, g, zero), jnp.where(left, zero, g)], axis=0)

    for p in range(pairs):
        products = dot(x[:, p * 2 * size:(p + 1) * 2 * size], stacked(p), NT)
        for q in range(2):
            h = 2 * p + q
            spans = running_t[h:h + 1, :] - shifted[:, h:h + 1]
            factor = jnp.exp(jnp.where(keep, spans, -1e30))
            grow[h] = factor
            form = form + factor * products[:, q * rows:(q + 1) * rows]
    cut = width // n_out
    packed = cut // 2
    taken = min(packed, 128)
    for c in range(width // 128):
        turned = jnp.transpose(hidden[:, c * 128:(c + 1) * 128])
        for r in range(0, 128, taken):
            group, inside = divmod(c * 128 + r, cut)
            to = group * packed + inside % packed
            hidden_t[to:to + taken, inside // packed * rows:(inside // packed + 1) * rows] = turned[r:r + taken]

    each_far(lambda k, o: far_copy(W_FAR, k, w_far.at[me_out], w_far.at[lax.rem(me_out + n_out - k, n_out)], o).wait_recv())
    w = w_far[...].reshape(width, 2 * state)
    projected = dot(hidden[...], w)
    projected_t = jnp.transpose(projected)
    proj_hi, proj_lo = split(projected_t)
    b_t = jnp.concatenate([proj_hi[:state], proj_lo[:state]], axis=0)
    c_t = jnp.concatenate([proj_hi[state:], proj_lo[state:]], axis=0)

    def rows_of(way):
        return slice(8 + state, 8 + 2 * state) if way else slice(0, 8 + state)

    def state_rows(way, first=8):
        return slice(first + way * state, first + (way + 1) * state)

    def lanes_of(side, t):
        return pl.ds(pl.multiple_of((t * 2 + side) * part, part), part)

    def side_lanes(ref, side):
        return jnp.concatenate([ref[:, lanes_of(side, t)] for t in range(n_chip)], axis=1)

    def own_half(way, side):
        which = c_t if way else b_t
        values, rests = (gw_hi, gw_lo) if way else (xw_hi, xw_lo)
        both = dot(which, side_lanes(values, side))
        made = both[:state] + both[state:] + dot(which[:state], side_lanes(rests, side))
        for t in range(n_chip):
            c_send[side, t, state_rows(way), :] = made[:, t * part:(t + 1) * part]

    def core_out(way, k, t):
        return near_copy(C_OUT + way, k, c_send.at[other, t, rows_of(way)], c_recv.at[t, rows_of(way)], chip * 2 + other)

    def chip_out(way, k, t, source):
        return near_copy(S_OUT + way, k, s_send.at[t, rows_of(way)], s_recv.at[source, rows_of(way)], t * 2 + core)

    def each_slice(act):
        lax.fori_loop(1, n_chip + 1, lambda k, c: (act(k, lax.rem(chip + k, n_chip)), c)[1], 0)

    def give(way):
        own_half(way, other)
        each_slice(lambda k, t: core_out(way, k, t).start())

    first_core = core == 0

    def join(way):
        def one(k, t):
            core_out(way, k, t).wait_recv()
            own_total, other_total = c_send[core, t, :1, :], c_recv[t, :1, :]
            ones = jnp.ones_like(own_total)
            own_factor, other_factor = jnp.exp(other_total), jnp.exp(own_total)
            own_is_far = first_core if way == 0 else jnp.logical_not(first_core)
            at = state_rows(way)
            s_send[t, at, :] = (
                jnp.where(own_is_far, own_factor, ones) * c_send[core, t, at, :]
                + jnp.where(own_is_far, ones, other_factor) * c_recv[t, at, :]
            )
            if way == 0:
                s_send[t, :8, :] = c_send[core, t, :8, :] + c_recv[t, :8, :]

            @pl.when(k < n_chip)
            def _():
                chip_out(way, k, t, chip).start()

            @pl.when(k == n_chip)
            def _():
                s_recv[t, rows_of(way)] = s_send[t, rows_of(way)]

        each_slice(one)

    give(0)
    own_half(0, core)
    give(1)
    join(0)
    own_half(1, core)
    join(1)

    b_rows, c_rows = projected[:, :state], projected[:, state:]
    scores = dot3(b_rows, c_rows, NT)
    for p in range(pairs):
        mixed = jnp.concatenate([grow[2 * p] * scores, grow[2 * p + 1] * scores], axis=1).astype(BF16)
        gx[:, p * 2 * size:(p + 1) * 2 * size] = dot(mixed, stacked(p))
    near_b = dot3(form, c_rows)
    near_c = dot3(jnp.transpose(form), b_rows)

    servers = n_out // 2

    def far_send(q, k, o):
        @pl.when(o // servers == q)
        def _():
            far_copy(S_FAR, k, o_send.at[o], o_recv.at[me_out], o).start()

    def far_step(forward):
        o_recv[me_out] = o_send[me_out]
        each_far(lambda k, o: far_copy(S_FAR, k, o_send.at[o], o_recv.at[lax.rem(me_out + n_out - k, n_out)], o).wait_recv())
        held = jnp.zeros((far, part), F32)
        for k in range(n_out):
            at = k if forward else n_out - 1 - k
            o_back[at] = held
            held = held * jnp.exp(o_recv[at, far:far + 1, :]) + o_recv[at, :far, :]
        each_far(lambda k, o: far_copy(S_BACK, k, o_back.at[o], carry.at[me_out], o).start())
        carry[me_out] = o_back[me_out]

    for way in range(WAYS):
        each_chip(lambda k, t: chip_out(way, k, t, lax.rem(chip + n_chip - k, n_chip)).wait_recv())
        if way == 0:
            totals = [s_recv[k, :1, :] for k in range(n_chip)]
            after, before = jnp.zeros((1, part), F32), jnp.zeros((1, part), F32)
            ahead, behind = [None] * n_chip, [None] * n_chip
            for k in range(n_chip):
                ahead[k], behind[n_chip - 1 - k] = jnp.exp(before), jnp.exp(after)
                before = before + totals[k]
                after = after + totals[n_chip - 1 - k]
            steps = [jnp.exp(t) for t in totals]
        held = jnp.zeros((state, part), F32)
        for k in range(n_chip - 1, -1, -1) if way else range(n_chip):
            prefix[k, state_rows(way, 0), :] = held
            held = held * steps[k] + s_recv[k, state_rows(way), :]
        for j in range(servers):
            o_send[way * servers + j, :far, :] = held[j * far:(j + 1) * far]
            o_send[way * servers + j, far:, :] = jnp.broadcast_to(before, (8, part))
        each_far(functools.partial(far_send, way))
    for forward in (True, False):
        pl.when((me_out < n_out // 2) == forward)(functools.partial(far_step, forward))

    def back_wait(q, k, o):
        source = lax.rem(me_out + n_out - k, n_out)

        @pl.when(source // servers == q)
        def _():
            far_copy(S_BACK, k, o_back.at[o], carry.at[source], o).wait_recv()

    def home_copy(way, k, t, source):
        at = state_rows(way, 0)
        return near_copy(S_HOME + way, k, s_back.at[t, at], s_home.at[source, at], t * 2 + core)

    for way in range(WAYS):
        each_far(functools.partial(back_wait, way))
        carried = jnp.concatenate([carry[way * servers + j] for j in range(servers)], axis=0)
        reach = behind if way else ahead
        at = state_rows(way, 0)
        for k in range(n_chip):
            s_back[k, at, :] = prefix[k, at, :] + reach[k] * carried
        each_chip(lambda k, t: home_copy(way, k, t, chip).start())
        s_home[chip, at, :] = s_back[chip, at, :]

    def core_home(way, k, side, t):
        at = state_rows(way, 0)
        return near_copy(C_HOME + way, k, c_back.at[t, at], states.at[side, t, at], chip * 2 + other)

    def use_half(way, side, sum_):
        values, rests = (xw_hi, xw_lo) if way else (gw_hi, gw_lo)
        got = jnp.concatenate([states[side, t, state_rows(way, 0), :] for t in range(n_chip)], axis=1)
        got_hi, got_lo = split(got)
        both = dot(side_lanes(values, side), jnp.concatenate([got_hi, got_lo], axis=0), NT)
        return sum_ + both[:, :state] + both[:, state:] + dot(side_lanes(rests, side), got_hi, NT)

    def source_of(k):
        return lax.rem(chip + n_chip - k, n_chip)

    def share(way, k):
        t = source_of(k)
        at, tall = state_rows(way, 0), state_rows(way)
        got = s_home[t, at, :]
        by_own = jnp.exp(c_send[core, t, :1, :]) * got + c_send[core, t, tall, :]
        by_other = jnp.exp(c_recv[t, :1, :]) * got + c_recv[t, tall, :]
        comes_first = first_core if way == 0 else jnp.logical_not(first_core)
        states[core, t, at, :] = jnp.where(comes_first, got, by_other)
        c_back[t, at, :] = jnp.where(comes_first, by_own, got)
        core_home(way, k, core, t).start()

    def term_copy(way, k, o, source):
        return far_copy(G_FAR + way, k, g_send.at[way, o], g_recv.at[way, source], o)

    def send_term(way, low):
        zero = jnp.zeros_like(low)
        pair = jnp.concatenate(
            [jnp.concatenate([low, zero], axis=1), jnp.concatenate([zero, low], axis=1)], axis=0
        )
        term = (dot(hidden_t[...], pair) * scale).astype(BF16)
        for o in range(n_out):
            g_send[way, o] = term[o * packed:(o + 1) * packed]
        each_far(lambda k, o: term_copy(way, k, o, me_out).start())
        g_recv[way, me_out] = g_send[way, me_out]

    sums = []
    for way, near in enumerate((near_c, near_b)):
        def share_arrived(k, t):
            source = source_of(k)
            home_copy(way, k, source, source).wait_recv()
            share(way, k)

        share(way, 0)
        each_chip(share_arrived)
        sum_ = use_half(way, core, near)
        each_slice(lambda k, t: core_home(way, k - 1, other, source_of(k - 1)).wait_recv())
        sums.append(use_half(way, other, sum_).astype(BF16))
        send_term(way, sums[way])
    d_low = jnp.concatenate(sums[::-1], axis=1)

    gh[...] = dot(d_low, w, NT)
    store_gh = pltpu.make_async_copy(gh, gh_hbm, load_sem.at[0])
    store_gh.start()

    halves = []
    for way in range(WAYS):
        each_far(lambda k, o: term_copy(way, k, o, lax.rem(me_out + n_out - k, n_out)).wait_recv())
        halves.append(functools.reduce(lambda a, b: a + b, [g_recv[way, o].astype(F32) for o in range(n_out)]))
    g_sum[:packed] = jnp.concatenate([halves[1][:, :state], halves[0][:, :state]], axis=1)
    g_sum[packed:] = jnp.concatenate([halves[1][:, state:], halves[0][:, state:]], axis=1)

    def owned(i):
        return g_sum.at[pl.ds(pl.multiple_of(i // per_tile * tile, tile), tile), :]

    each_near(lambda k, i: near_copy(G_NEAR, k, owned(i), g_near.at[me_in], i).start())
    g_near[me_in] = g_sum[pl.ds(pl.multiple_of(me_in // per_tile * tile, tile), tile), :]

    b_hi, b_lo = split(b_rows)
    b_three = jnp.concatenate([b_hi, b_lo, b_hi], axis=1)
    for i in range(n_in):
        at = slice(i * part, (i + 1) * part)
        got_hi, got_lo = split(states[i % 2, i // 2, state:, :])
        gx[:, at] = gx[:, at] + spread[:, at] * dot(b_three, jnp.concatenate([got_hi, got_hi, got_lo], axis=0))
    store_gx = pltpu.make_async_copy(gx, gx_hbm, load_sem.at[1])
    store_gx.start()

    each_near(lambda k, i: near_copy(G_NEAR, k, owned(i), g_near.at[lax.rem(me_in + n_in - k, n_in)], i).wait_recv())
    summed = functools.reduce(lambda a, b: a + b, [g_near[i] for i in range(n_in)])
    mine = summed[:own_rows]
    for q in range(1, per_tile):
        mine = jnp.where(lax.rem(me_in, per_tile) == q, summed[q * own_rows:(q + 1) * own_rows], mine)
    gp_ref[...] = mine

    each_near(lambda k, i: near_copy(W_NEAR, k, w_near.at[me_in], w_near.at[me_in], i).wait_send())
    each_far(lambda k, o: far_copy(W_FAR, k, w_far.at[me_out], w_far.at[me_out], o).wait_send())
    for way in range(WAYS):
        each_slice(lambda k, t: core_out(way, k, t).wait_send())
        each_chip(lambda k, t: chip_out(way, k, t, chip).wait_send())
        each_chip(lambda k, t: home_copy(way, k, t, chip).wait_send())
        each_slice(lambda k, t: core_home(way, k - 1, core, source_of(k - 1)).wait_send())
    each_far(lambda k, o: far_copy(S_FAR, k, o_send.at[o], o_recv.at[me_out], o).wait_send())
    each_far(lambda k, o: far_copy(S_BACK, k, o_back.at[o], carry.at[me_out], o).wait_send())
    for way in range(WAYS):
        each_far(lambda k, o: term_copy(way, k, o, me_out).wait_send())
    each_near(lambda k, i: near_copy(G_NEAR, k, owned(i), g_near.at[me_in], i).wait_send())
    store_gh.wait()
    store_gx.wait()


def write_out(gx_from, gh_from, gp_from, gx_to, gh_to, gp_to, gx, gh, gp, sem):
    pieces = gx.shape[1]
    moves = [(gp_from, gp, gp_to)]
    for q in range(gx.shape[0]):
        at = slice(q * pieces, (q + 1) * pieces)
        moves.append((gx_from.at[at], gx.at[q], gx_to.at[at]))
        moves.append((gh_from.at[at], gh.at[q], gh_to.at[at]))
    reads = [pltpu.make_async_copy(m[0], m[1], sem.at[0, k]) for k, m in enumerate(moves)]
    writes = [pltpu.make_async_copy(m[1], m[2], sem.at[1, k]) for k, m in enumerate(moves)]
    for read in reads:
        read.start()
    for read, write in zip(reads, writes):
        read.wait()
        write.start()
    for write in writes:
        write.wait()


def per_device(hidden, x_act, dt_step, log_decay, w_bc, grad_y):
    n_out, n_in = lax.axis_size("outer"), lax.axis_size("inner")
    rows, width = hidden.shape
    lanes = x_act.shape[1]
    heads = dt_step.shape[1]
    own_rows, columns = w_bc.shape
    part = lanes // n_in
    far = columns // n_out
    tile = max(8, own_rows)
    most = max(n_out, n_in)
    scale = 1.0 / math.sqrt(rows * n_out * n_in)
    anywhere = pl.BlockSpec(memory_space=pl.ANY)
    vmem = pl.BlockSpec(memory_space=pltpu.VMEM)
    results = pl.pallas_call(
        functools.partial(kernel, scale, n_out, n_in),
        out_shape=(
            jax.ShapeDtypeStruct((rows, lanes), F32),
            jax.ShapeDtypeStruct((rows, width), F32),
            jax.ShapeDtypeStruct((own_rows, columns), F32),
        ),
        in_specs=[anywhere, anywhere, anywhere, anywhere, vmem, anywhere],
        out_specs=(anywhere, anywhere, vmem),
        scratch_shapes=[
            pltpu.VMEM((rows, width), BF16),
            pltpu.VMEM((rows, lanes), BF16),
            pltpu.VMEM((rows, lanes), BF16),
            pltpu.VMEM((heads, rows), F32),
            pltpu.VMEM((heads, rows), F32),
            pltpu.VMEM((width // 2, 2 * rows), BF16),
            pltpu.VMEM((rows, lanes), F32),
            pltpu.VMEM((rows, width), F32),
            pltpu.VMEM((n_in, tile, columns), F32),
            pltpu.VMEM((n_out, width // n_out, columns), BF16),
            pltpu.VMEM((heads, rows, rows), F32),
            pltpu.VMEM((rows, lanes), F32),
            pltpu.VMEM((rows, lanes), BF16),
            pltpu.VMEM((rows, lanes), BF16),
            pltpu.VMEM((rows, lanes), BF16),
            pltpu.VMEM((rows, lanes), BF16),
            pltpu.VMEM((2, n_in // 2, columns + 8, part), F32),
            pltpu.VMEM((n_in // 2, columns + 8, part), F32),
            pltpu.VMEM((n_in // 2, columns + 8, part), F32),
            pltpu.VMEM((n_in // 2, columns + 8, part), F32),
            pltpu.VMEM((n_in // 2, columns, part), F32),
            pltpu.VMEM((n_out, far + 8, part), F32),
            pltpu.VMEM((n_out, far + 8, part), F32),
            pltpu.VMEM((n_out, far, part), F32),
            pltpu.VMEM((n_out, far, part), F32),
            pltpu.VMEM((n_in // 2, columns, part), F32),
            pltpu.VMEM((n_in // 2, columns, part), F32),
            pltpu.VMEM((n_in // 2, columns, part), F32),
            pltpu.VMEM((2, n_in // 2, columns, part), F32),
            pltpu.VMEM((2, n_out, width // n_out // 2, columns), BF16),
            pltpu.VMEM((2, n_out, width // n_out // 2, columns), BF16),
            pltpu.VMEM((width // n_out, columns), F32),
            pltpu.VMEM((n_in, tile, columns), F32),
            pltpu.SemaphoreType.DMA((5,)),
            pltpu.SemaphoreType.DMA((PHASES, most)),
            pltpu.SemaphoreType.DMA((PHASES, most)),
        ],
        compiler_params=pltpu.CompilerParams(
            collective_id=0, has_side_effects=True, vmem_limit_bytes=60 * 1024 * 1024
        ),
        cost_estimate=pl.CostEstimate(flops=10**9, bytes_accessed=3 * 10**6, transcendentals=10**6),
    )(hidden, x_act, dt_step.T, log_decay.T, w_bc, grad_y)
    pieces = rows // 4
    return pl.pallas_call(
        write_out,
        out_shape=tuple(jax.ShapeDtypeStruct(r.shape, r.dtype) for r in results),
        in_specs=[anywhere] * 3,
        out_specs=(anywhere,) * 3,
        scratch_shapes=[
            pltpu.VMEM((4, pieces, lanes), F32),
            pltpu.VMEM((4, pieces, width), F32),
            pltpu.VMEM((own_rows, columns), F32),
            pltpu.SemaphoreType.DMA((2, 9)),
        ],
        compiler_params=pltpu.CompilerParams(vmem_limit_bytes=60 * 1024 * 1024),
    )(*results)


def solution(mesh):
    spec = P(("outer", "inner"), None)
    return jax.shard_map(
        per_device, mesh=mesh, in_specs=(spec,) * 6, out_specs=(spec,) * 3, check_vma=False
    )
```

```python
import functools
import math

import jax
import jax.numpy as jnp
from jax import lax
from jax.experimental import pallas as pl
from jax.experimental.pallas import tpu as pltpu
from jax.sharding import PartitionSpec as P

BF16 = jnp.bfloat16
F32 = jnp.float32
MESH = pl.DeviceIdType.MESH
HIGH = lax.Precision.HIGHEST

NN = (((1,), (0,)), ((), ()))
NT = (((1,), (1,)), ((), ()))

W_NEAR, W_FAR, S_FAR, S_BACK, G_NEAR, S_OUT = range(6)
WAYS = 2
S_HOME = S_OUT + WAYS
C_OUT = S_HOME + WAYS
C_HOME = C_OUT + WAYS
G_FAR = C_HOME + WAYS
PHASES = G_FAR + WAYS


def dot(a, b, dims=NN):
    return lax.dot_general(a, b, dims, preferred_element_type=F32)


def split(value):
    high = value.astype(BF16)
    return high, (value - high.astype(F32)).astype(BF16)


def dot3(a, b, dims=NN):
    a_high, a_low = split(a)
    b_high, b_low = split(b)
    return dot(a_high, b_high, dims) + dot(a_high, b_low, dims) + dot(a_low, b_high, dims)


def iota(shape, axis):
    return lax.broadcasted_iota(jnp.int32, shape, axis)


def kernel(
    scale, n_out, n_in,
    hidden_hbm, x_hbm, dt_hbm, decay_hbm, w_ref, gy_hbm,
    gx_hbm, gh_hbm, gp_ref,
    hidden, x, gy, dt_ref, decay_ref, hidden_t, gx, gh,
    w_near, w_far, grow, spread, xw_hi, xw_lo, gw_hi, gw_lo,
    c_send, c_recv, s_send, s_recv, prefix, o_send, o_recv, o_back, carry, s_back, s_home, c_back, states,
    g_send, g_recv, g_sum, g_near,
    load_sem, send_sem, recv_sem,
):
    me_out, me_in = lax.axis_index("outer"), lax.axis_index("inner")
    rows, width = hidden.shape
    lanes = x.shape[1]
    heads = dt_ref.shape[0]
    size = lanes // heads
    state = w_far.shape[2] // 2
    part = lanes // n_in
    far = 2 * state // n_out
    pairs = heads // 2
    n_chip = n_in // 2
    chip, core = me_in // 2, lax.rem(me_in, 2)
    other = 1 - core

    loads = [
        pltpu.make_async_copy(source, target, load_sem.at[k])
        for k, (source, target) in enumerate(
            ((decay_hbm, decay_ref), (dt_hbm, dt_ref), (x_hbm, x), (gy_hbm, gy), (hidden_hbm, hidden))
        )
    ]
    for load in loads:
        load.start()

    barrier = pltpu.get_barrier_semaphore()

    def each_near(act):
        lax.fori_loop(1, n_in, lambda k, c: (act(k, lax.rem(me_in + k, n_in)), c)[1], 0)

    def each_chip(act):
        lax.fori_loop(1, n_chip, lambda k, c: (act(k, lax.rem(chip + k, n_chip)), c)[1], 0)

    def each_far(act):
        lax.fori_loop(1, n_out, lambda k, c: (act(k, lax.rem(me_out + k, n_out)), c)[1], 0)

    def greet(*place):
        pl.semaphore_signal(barrier, inc=1, device_id=place, device_id_type=MESH)

    each_near(lambda k, i: greet(me_out, i))
    each_far(lambda k, o: greet(o, me_in))

    def near_copy(phase, k, source, target, i):
        return pltpu.make_async_remote_copy(
            src_ref=source, dst_ref=target, send_sem=send_sem.at[phase, k], recv_sem=recv_sem.at[phase, k],
            device_id=(me_out, i), device_id_type=MESH,
        )

    def far_copy(phase, k, source, target, o):
        return pltpu.make_async_remote_copy(
            src_ref=source, dst_ref=target, send_sem=send_sem.at[phase, k], recv_sem=recv_sem.at[phase, k],
            device_id=(o, me_in), device_id_type=MESH,
        )

    own_rows = w_ref.shape[0]
    tile = w_near.shape[1]
    per_tile = tile // own_rows
    own_w = jnp.concatenate([w_ref[...].astype(F32)] * per_tile, axis=0)
    own_w = jnp.where(iota(own_w.shape, 0) // own_rows == lax.rem(me_in, per_tile), own_w, 0.0)
    w_near[me_in] = own_w

    pl.semaphore_wait(barrier, n_in + n_out - 2)
    each_near(lambda k, i: near_copy(W_NEAR, k, w_near.at[me_in], w_near.at[me_in], i).start())

    loads[0].wait()
    loads[1].wait()
    upto = (iota((rows, rows), 0) <= iota((rows, rows), 1)).astype(F32)
    running_t = lax.dot_general(decay_ref[...], upto, NN, precision=HIGH, preferred_element_type=F32)
    dt_t = dt_ref[...]
    total_t = jnp.broadcast_to(running_t[:, rows - 1:], running_t.shape)
    columns = jnp.transpose(jnp.concatenate(
        [dt_t * jnp.exp(total_t - running_t), jnp.exp(running_t), total_t, running_t - jnp.log(dt_t)], axis=0
    ))
    shifted = columns[:, 3 * heads:]
    stack = jnp.concatenate(
        [columns[:, :heads], columns[:, heads:2 * heads], columns[:8, 2 * heads:3 * heads]], axis=0
    )
    high = stack.astype(BF16)
    rest = stack - high.astype(F32)
    middle = rest.astype(BF16)
    low = (rest - middle.astype(F32)).astype(BF16)
    stack = jnp.concatenate([high, middle, low], axis=1)
    for load in loads[2:]:
        load.wait()
    for c in range(lanes // 256):
        at = slice(c * 256, (c + 1) * 256)
        chosen = lax.rem(iota((3 * heads, 256), 0), heads) == (iota((3 * heads, 256), 1) + c * 256) // size
        wide = dot(stack, jnp.where(chosen, 1.0, 0.0).astype(BF16))
        spread[:, at] = wide[:rows]
        xw_hi[:, at], xw_lo[:, at] = split(x[:, at].astype(F32) * wide[:rows])
        gw_hi[:, at], gw_lo[:, at] = split(gy[:, at].astype(F32) * wide[rows:2 * rows])
        for q in range(max(1, 256 // part)):
            lane = c * 256 + q * part
            cut = min(part, 256)
            i = lane // part
            c_send[i % 2, i // 2, :8, lane % part:lane % part + cut] = wide[2 * rows:, q * part:q * part + cut]

    each_near(lambda k, i: near_copy(W_NEAR, k, w_near.at[me_in], w_near.at[lax.rem(me_in + n_in - k, n_in)], i).wait_recv())
    block = [
        functools.reduce(lambda a, b: a + b, [w_near[t * per_tile + q] for q in range(per_tile)])
        for t in range(n_in // per_tile)
    ]
    w_far[me_out] = jnp.concatenate(block, axis=0).astype(BF16)
    each_far(lambda k, o: far_copy(W_FAR, k, w_far.at[me_out], w_far.at[me_out], o).start())

    left = iota((rows, 2 * size), 1) < size
    keep = iota((rows, rows), 0) <= iota((rows, rows), 1)
    form = jnp.zeros((rows, rows), F32)

    def stacked(p):
        g = gy[:, p * 2 * size:(p + 1) * 2 * size]
        zero = jnp.zeros_like(g)
        return jnp.concatenate([jnp.where(left, g, zero), jnp.where(left, zero, g)], axis=0)

    for p in range(pairs):
        products = dot(x[:, p * 2 * size:(p + 1) * 2 * size], stacked(p), NT)
        for q in range(2):
            h = 2 * p + q
            spans = running_t[h:h + 1, :] - shifted[:, h:h + 1]
            factor = jnp.exp(jnp.where(keep, spans, -1e30))
            grow[h] = factor
            form = form + factor * products[:, q * rows:(q + 1) * rows]
    cut = width // n_out
    packed = cut // 2
    taken = min(packed, 128)
    for c in range(width // 128):
        turned = jnp.transpose(hidden[:, c * 128:(c + 1) * 128])
        for r in range(0, 128, taken):
            group, inside = divmod(c * 128 + r, cut)
            to = group * packed + inside % packed
            hidden_t[to:to + taken, inside // packed * rows:(inside // packed + 1) * rows] = turned[r:r + taken]

    each_far(lambda k, o: far_copy(W_FAR, k, w_far.at[me_out], w_far.at[lax.rem(me_out + n_out - k, n_out)], o).wait_recv())
    w = w_far[...].reshape(width, 2 * state)
    projected = dot(hidden[...], w)
    projected_t = jnp.transpose(projected)
    proj_hi, proj_lo = split(projected_t)
    b_t = jnp.concatenate([proj_hi[:state], proj_lo[:state]], axis=0)
    c_t = jnp.concatenate([proj_hi[state:], proj_lo[state:]], axis=0)

    def rows_of(way):
        return slice(8 + state, 8 + 2 * state) if way else slice(0, 8 + state)

    def state_rows(way, first=8):
        return slice(first + way * state, first + (way + 1) * state)

    def lanes_of(side, t):
        return pl.ds(pl.multiple_of((t * 2 + side) * part, part), part)

    def side_lanes(ref, side):
        return jnp.concatenate([ref[:, lanes_of(side, t)] for t in range(n_chip)], axis=1)

    def own_half(way, side):
        which = c_t if way else b_t
        values, rests = (gw_hi, gw_lo) if way else (xw_hi, xw_lo)
        both = dot(which, side_lanes(values, side))
        made = both[:state] + both[state:] + dot(which[:state], side_lanes(rests, side))
        for t in range(n_chip):
            c_send[side, t, state_rows(way), :] = made[:, t * part:(t + 1) * part]

    def core_out(way, k, t):
        return near_copy(C_OUT + way, k, c_send.at[other, t, rows_of(way)], c_recv.at[t, rows_of(way)], chip * 2 + other)

    def chip_out(way, k, t, source):
        return near_copy(S_OUT + way, k, s_send.at[t, rows_of(way)], s_recv.at[source, rows_of(way)], t * 2 + core)

    def each_slice(act):
        lax.fori_loop(1, n_chip + 1, lambda k, c: (act(k, lax.rem(chip + k, n_chip)), c)[1], 0)

    def give(way):
        own_half(way, other)
        each_slice(lambda k, t: core_out(way, k, t).start())

    first_core = core == 0

    def join(way):
        def one(k, t):
            core_out(way, k, t).wait_recv()
            own_total, other_total = c_send[core, t, :1, :], c_recv[t, :1, :]
            ones = jnp.ones_like(own_total)
            own_factor, other_factor = jnp.exp(other_total), jnp.exp(own_total)
            own_is_far = first_core if way == 0 else jnp.logical_not(first_core)
            at = state_rows(way)
            s_send[t, at, :] = (
                jnp.where(own_is_far, own_factor, ones) * c_send[core, t, at, :]
                + jnp.where(own_is_far, ones, other_factor) * c_recv[t, at, :]
            )
            if way == 0:
                s_send[t, :8, :] = c_send[core, t, :8, :] + c_recv[t, :8, :]

            @pl.when(k < n_chip)
            def _():
                chip_out(way, k, t, chip).start()

            @pl.when(k == n_chip)
            def _():
                s_recv[t, rows_of(way)] = s_send[t, rows_of(way)]

        each_slice(one)

    give(0)
    own_half(0, core)
    give(1)
    join(0)
    own_half(1, core)
    join(1)

    b_rows, c_rows = projected[:, :state], projected[:, state:]
    scores = dot3(b_rows, c_rows, NT)
    for p in range(pairs):
        mixed = jnp.concatenate([grow[2 * p] * scores, grow[2 * p + 1] * scores], axis=1).astype(BF16)
        gx[:, p * 2 * size:(p + 1) * 2 * size] = dot(mixed, stacked(p))
    near_b = dot3(form, c_rows)
    near_c = dot3(jnp.transpose(form), b_rows)

    servers = n_out // 2

    def far_send(q, k, o):
        @pl.when(o // servers == q)
        def _():
            far_copy(S_FAR, k, o_send.at[o], o_recv.at[me_out], o).start()

    def far_step(forward):
        o_recv[me_out] = o_send[me_out]
        each_far(lambda k, o: far_copy(S_FAR, k, o_send.at[o], o_recv.at[lax.rem(me_out + n_out - k, n_out)], o).wait_recv())
        held = jnp.zeros((far, part), F32)
        for k in range(n_out):
            at = k if forward else n_out - 1 - k
            o_back[at] = held
            held = held * jnp.exp(o_recv[at, far:far + 1, :]) + o_recv[at, :far, :]
        each_far(lambda k, o: far_copy(S_BACK, k, o_back.at[o], carry.at[me_out], o).start())
        carry[me_out] = o_back[me_out]

    for way in range(WAYS):
        each_chip(lambda k, t: chip_out(way, k, t, lax.rem(chip + n_chip - k, n_chip)).wait_recv())
        if way == 0:
            totals = [s_recv[k, :1, :] for k in range(n_chip)]
            after, before = jnp.zeros((1, part), F32), jnp.zeros((1, part), F32)
            ahead, behind = [None] * n_chip, [None] * n_chip
            for k in range(n_chip):
                ahead[k], behind[n_chip - 1 - k] = jnp.exp(before), jnp.exp(after)
                before = before + totals[k]
                after = after + totals[n_chip - 1 - k]
            steps = [jnp.exp(t) for t in totals]
        held = jnp.zeros((state, part), F32)
        for k in range(n_chip - 1, -1, -1) if way else range(n_chip):
            prefix[k, state_rows(way, 0), :] = held
            held = held * steps[k] + s_recv[k, state_rows(way), :]
        for j in range(servers):
            o_send[way * servers + j, :far, :] = held[j * far:(j + 1) * far]
            o_send[way * servers + j, far:, :] = jnp.broadcast_to(before, (8, part))
        each_far(functools.partial(far_send, way))
    for forward in (True, False):
        pl.when((me_out < n_out // 2) == forward)(functools.partial(far_step, forward))

    def back_wait(q, k, o):
        source = lax.rem(me_out + n_out - k, n_out)

        @pl.when(source // servers == q)
        def _():
            far_copy(S_BACK, k, o_back.at[o], carry.at[source], o).wait_recv()

    def home_copy(way, k, t, source):
        at = state_rows(way, 0)
        return near_copy(S_HOME + way, k, s_back.at[t, at], s_home.at[source, at], t * 2 + core)

    for way in range(WAYS):
        each_far(functools.partial(back_wait, way))
        carried = jnp.concatenate([carry[way * servers + j] for j in range(servers)], axis=0)
        reach = behind if way else ahead
        at = state_rows(way, 0)
        for k in range(n_chip):
            s_back[k, at, :] = prefix[k, at, :] + reach[k] * carried
        each_chip(lambda k, t: home_copy(way, k, t, chip).start())
        s_home[chip, at, :] = s_back[chip, at, :]

    def core_home(way, k, side, t):
        at = state_rows(way, 0)
        return near_copy(C_HOME + way, k, c_back.at[t, at], states.at[side, t, at], chip * 2 + other)

    def use_half(way, side, sum_):
        values, rests = (xw_hi, xw_lo) if way else (gw_hi, gw_lo)
        got = jnp.concatenate([states[side, t, state_rows(way, 0), :] for t in range(n_chip)], axis=1)
        got_hi, got_lo = split(got)
        both = dot(side_lanes(values, side), jnp.concatenate([got_hi, got_lo], axis=0), NT)
        return sum_ + both[:, :state] + both[:, state:] + dot(side_lanes(rests, side), got_hi, NT)

    def source_of(k):
        return lax.rem(chip + n_chip - k, n_chip)

    def share(way, k):
        t = source_of(k)
        at, tall = state_rows(way, 0), state_rows(way)
        got = s_home[t, at, :]
        by_own = jnp.exp(c_send[core, t, :1, :]) * got + c_send[core, t, tall, :]
        by_other = jnp.exp(c_recv[t, :1, :]) * got + c_recv[t, tall, :]
        comes_first = first_core if way == 0 else jnp.logical_not(first_core)
        states[core, t, at, :] = jnp.where(comes_first, got, by_other)
        c_back[t, at, :] = jnp.where(comes_first, by_own, got)
        core_home(way, k, core, t).start()

    def term_copy(way, k, o, source):
        return far_copy(G_FAR + way, k, g_send.at[way, o], g_recv.at[way, source], o)

    def send_term(way, low):
        zero = jnp.zeros_like(low)
        pair = jnp.concatenate(
            [jnp.concatenate([low, zero], axis=1), jnp.concatenate([zero, low], axis=1)], axis=0
        )
        term = (dot(hidden_t[...], pair) * scale).astype(BF16)
        for o in range(n_out):
            g_send[way, o] = term[o * packed:(o + 1) * packed]
        each_far(lambda k, o: term_copy(way, k, o, me_out).start())
        g_recv[way, me_out] = g_send[way, me_out]

    sums = []
    for way, near in enumerate((near_c, near_b)):
        def share_arrived(k, t):
            source = source_of(k)
            home_copy(way, k, source, source).wait_recv()
            share(way, k)

        share(way, 0)
        each_chip(share_arrived)
        sum_ = use_half(way, core, near)
        each_slice(lambda k, t: core_home(way, k - 1, other, source_of(k - 1)).wait_recv())
        sums.append(use_half(way, other, sum_).astype(BF16))
        send_term(way, sums[way])
    d_low = jnp.concatenate(sums[::-1], axis=1)

    gh[...] = dot(d_low, w, NT)
    store_gh = pltpu.make_async_copy(gh, gh_hbm, load_sem.at[0])
    store_gh.start()

    b_hi, b_lo = split(b_rows)
    b_three = jnp.concatenate([b_hi, b_lo, b_hi], axis=1)
    for i in range(n_in):
        at = slice(i * part, (i + 1) * part)
        got_hi, got_lo = split(states[i % 2, i // 2, state:, :])
        gx[:, at] = gx[:, at] + spread[:, at] * dot(b_three, jnp.concatenate([got_hi, got_hi, got_lo], axis=0))
    store_gx = pltpu.make_async_copy(gx, gx_hbm, load_sem.at[1])
    store_gx.start()

    halves = []
    for way in range(WAYS):
        each_far(lambda k, o: term_copy(way, k, o, lax.rem(me_out + n_out - k, n_out)).wait_recv())
        halves.append(functools.reduce(lambda a, b: a + b, [g_recv[way, o].astype(F32) for o in range(n_out)]))
    g_sum[:packed] = jnp.concatenate([halves[1][:, :state], halves[0][:, :state]], axis=1)
    g_sum[packed:] = jnp.concatenate([halves[1][:, state:], halves[0][:, state:]], axis=1)

    def owned(i):
        return g_sum.at[pl.ds(pl.multiple_of(i // per_tile * tile, tile), tile), :]

    each_near(lambda k, i: near_copy(G_NEAR, k, owned(i), g_near.at[me_in], i).start())
    g_near[me_in] = g_sum[pl.ds(pl.multiple_of(me_in // per_tile * tile, tile), tile), :]

    each_near(lambda k, i: near_copy(W_NEAR, k, w_near.at[me_in], w_near.at[me_in], i).wait_send())
    each_far(lambda k, o: far_copy(W_FAR, k, w_far.at[me_out], w_far.at[me_out], o).wait_send())
    for way in range(WAYS):
        each_slice(lambda k, t: core_out(way, k, t).wait_send())
        each_chip(lambda k, t: chip_out(way, k, t, chip).wait_send())
        each_chip(lambda k, t: home_copy(way, k, t, chip).wait_send())
        each_slice(lambda k, t: core_home(way, k - 1, core, source_of(k - 1)).wait_send())
    each_far(lambda k, o: far_copy(S_FAR, k, o_send.at[o], o_recv.at[me_out], o).wait_send())
    each_far(lambda k, o: far_copy(S_BACK, k, o_back.at[o], carry.at[me_out], o).wait_send())
    for way in range(WAYS):
        each_far(lambda k, o: term_copy(way, k, o, me_out).wait_send())
    each_near(lambda k, i: near_copy(G_NEAR, k, owned(i), g_near.at[lax.rem(me_in + n_in - k, n_in)], i).wait_recv())
    summed = functools.reduce(lambda a, b: a + b, [g_near[i] for i in range(n_in)])
    mine = summed[:own_rows]
    for q in range(1, per_tile):
        mine = jnp.where(lax.rem(me_in, per_tile) == q, summed[q * own_rows:(q + 1) * own_rows], mine)
    gp_ref[...] = mine

    each_near(lambda k, i: near_copy(G_NEAR, k, owned(i), g_near.at[me_in], i).wait_send())
    store_gh.wait()
    store_gx.wait()


def write_out(gx_from, gh_from, gp_from, gx_to, gh_to, gp_to, gx, gh, gp, sem):
    pieces = gx.shape[1]
    moves = [(gp_from, gp, gp_to)]
    for q in range(gx.shape[0]):
        at = slice(q * pieces, (q + 1) * pieces)
        moves.append((gx_from.at[at], gx.at[q], gx_to.at[at]))
        moves.append((gh_from.at[at], gh.at[q], gh_to.at[at]))
    reads = [pltpu.make_async_copy(m[0], m[1], sem.at[0, k]) for k, m in enumerate(moves)]
    writes = [pltpu.make_async_copy(m[1], m[2], sem.at[1, k]) for k, m in enumerate(moves)]
    for read in reads:
        read.start()
    for read, write in zip(reads, writes):
        read.wait()
        write.start()
    for write in writes:
        write.wait()


def per_device(hidden, x_act, dt_step, log_decay, w_bc, grad_y):
    n_out, n_in = lax.axis_size("outer"), lax.axis_size("inner")
    rows, width = hidden.shape
    lanes = x_act.shape[1]
    heads = dt_step.shape[1]
    own_rows, columns = w_bc.shape
    part = lanes // n_in
    far = columns // n_out
    tile = max(8, own_rows)
    most = max(n_out, n_in)
    scale = 1.0 / math.sqrt(rows * n_out * n_in)
    anywhere = pl.BlockSpec(memory_space=pl.ANY)
    vmem = pl.BlockSpec(memory_space=pltpu.VMEM)
    results = pl.pallas_call(
        functools.partial(kernel, scale, n_out, n_in),
        out_shape=(
            jax.ShapeDtypeStruct((rows, lanes), F32),
            jax.ShapeDtypeStruct((rows, width), F32),
            jax.ShapeDtypeStruct((own_rows, columns), F32),
        ),
        in_specs=[anywhere, anywhere, anywhere, anywhere, vmem, anywhere],
        out_specs=(anywhere, anywhere, vmem),
        scratch_shapes=[
            pltpu.VMEM((rows, width), BF16),
            pltpu.VMEM((rows, lanes), BF16),
            pltpu.VMEM((rows, lanes), BF16),
            pltpu.VMEM((heads, rows), F32),
            pltpu.VMEM((heads, rows), F32),
            pltpu.VMEM((width // 2, 2 * rows), BF16),
            pltpu.VMEM((rows, lanes), F32),
            pltpu.VMEM((rows, width), F32),
            pltpu.VMEM((n_in, tile, columns), F32),
            pltpu.VMEM((n_out, width // n_out, columns), BF16),
            pltpu.VMEM((heads, rows, rows), F32),
            pltpu.VMEM((rows, lanes), F32),
            pltpu.VMEM((rows, lanes), BF16),
            pltpu.VMEM((rows, lanes), BF16),
            pltpu.VMEM((rows, lanes), BF16),
            pltpu.VMEM((rows, lanes), BF16),
            pltpu.VMEM((2, n_in // 2, columns + 8, part), F32),
            pltpu.VMEM((n_in // 2, columns + 8, part), F32),
            pltpu.VMEM((n_in // 2, columns + 8, part), F32),
            pltpu.VMEM((n_in // 2, columns + 8, part), F32),
            pltpu.VMEM((n_in // 2, columns, part), F32),
            pltpu.VMEM((n_out, far + 8, part), F32),
            pltpu.VMEM((n_out, far + 8, part), F32),
            pltpu.VMEM((n_out, far, part), F32),
            pltpu.VMEM((n_out, far, part), F32),
            pltpu.VMEM((n_in // 2, columns, part), F32),
            pltpu.VMEM((n_in // 2, columns, part), F32),
            pltpu.VMEM((n_in // 2, columns, part), F32),
            pltpu.VMEM((2, n_in // 2, columns, part), F32),
            pltpu.VMEM((2, n_out, width // n_out // 2, columns), BF16),
            pltpu.VMEM((2, n_out, width // n_out // 2, columns), BF16),
            pltpu.VMEM((width // n_out, columns), F32),
            pltpu.VMEM((n_in, tile, columns), F32),
            pltpu.SemaphoreType.DMA((5,)),
            pltpu.SemaphoreType.DMA((PHASES, most)),
            pltpu.SemaphoreType.DMA((PHASES, most)),
        ],
        compiler_params=pltpu.CompilerParams(
            collective_id=0, has_side_effects=True, vmem_limit_bytes=60 * 1024 * 1024
        ),
        cost_estimate=pl.CostEstimate(flops=10**9, bytes_accessed=3 * 10**6, transcendentals=10**6),
    )(hidden, x_act, dt_step.T, log_decay.T, w_bc, grad_y)
    pieces = rows // 4
    return pl.pallas_call(
        write_out,
        out_shape=tuple(jax.ShapeDtypeStruct(r.shape, r.dtype) for r in results),
        in_specs=[anywhere] * 3,
        out_specs=(anywhere,) * 3,
        scratch_shapes=[
            pltpu.VMEM((4, pieces, lanes), F32),
            pltpu.VMEM((4, pieces, width), F32),
            pltpu.VMEM((own_rows, columns), F32),
            pltpu.SemaphoreType.DMA((2, 9)),
        ],
        compiler_params=pltpu.CompilerParams(vmem_limit_bytes=60 * 1024 * 1024),
    )(*results)


def solution(mesh):
    spec = P(("outer", "inner"), None)
    return jax.shard_map(
        per_device, mesh=mesh, in_specs=(spec,) * 6, out_specs=(spec,) * 3, check_vma=False
    )
```

```python
import functools
import math

import jax
import jax.numpy as jnp
from jax import lax
from jax.experimental import pallas as pl
from jax.experimental.pallas import tpu as pltpu
from jax.sharding import PartitionSpec as P

BF16 = jnp.bfloat16
F32 = jnp.float32
MESH = pl.DeviceIdType.MESH
HIGH = lax.Precision.HIGHEST

NN = (((1,), (0,)), ((), ()))
NT = (((1,), (1,)), ((), ()))

W_NEAR, W_FAR, S_FAR, S_BACK, G_NEAR, S_OUT = range(6)
WAYS = 2
S_HOME = S_OUT + WAYS
C_OUT = S_HOME + WAYS
C_HOME = C_OUT + WAYS
G_FAR = C_HOME + WAYS
PHASES = G_FAR + WAYS


def dot(a, b, dims=NN):
    return lax.dot_general(a, b, dims, preferred_element_type=F32)


def split(value):
    high = value.astype(BF16)
    return high, (value - high.astype(F32)).astype(BF16)


def dot3(a, b, dims=NN):
    a_high, a_low = split(a)
    b_high, b_low = split(b)
    return dot(a_high, b_high, dims) + dot(a_high, b_low, dims) + dot(a_low, b_high, dims)


def iota(shape, axis):
    return lax.broadcasted_iota(jnp.int32, shape, axis)


def kernel(
    scale, n_out, n_in,
    hidden_hbm, x_hbm, dt_hbm, decay_hbm, w_ref, gy_hbm,
    gx_hbm, gh_hbm, gp_ref,
    hidden, x, gy, dt_ref, decay_ref, hidden_t, gx, gh,
    w_near, w_far, grow, spread, xw_hi, xw_lo, gw_hi, gw_lo,
    c_send, c_recv, s_send, s_recv, prefix, o_send, o_recv, o_back, carry, s_back, s_home, c_back, states,
    g_send, g_recv, g_sum, g_near,
    load_sem, send_sem, recv_sem,
):
    me_out, me_in = lax.axis_index("outer"), lax.axis_index("inner")
    rows, width = hidden.shape
    lanes = x.shape[1]
    heads = dt_ref.shape[0]
    size = lanes // heads
    state = w_far.shape[2] // 2
    part = lanes // n_in
    far = 2 * state // n_out
    pairs = heads // 2
    n_chip = n_in // 2
    chip, core = me_in // 2, lax.rem(me_in, 2)
    other = 1 - core

    loads = [
        pltpu.make_async_copy(source, target, load_sem.at[k])
        for k, (source, target) in enumerate(
            ((decay_hbm, decay_ref), (dt_hbm, dt_ref), (x_hbm, x), (gy_hbm, gy), (hidden_hbm, hidden))
        )
    ]
    for load in loads:
        load.start()

    barrier = pltpu.get_barrier_semaphore()

    def each_near(act):
        lax.fori_loop(1, n_in, lambda k, c: (act(k, lax.rem(me_in + k, n_in)), c)[1], 0)

    def each_chip(act):
        lax.fori_loop(1, n_chip, lambda k, c: (act(k, lax.rem(chip + k, n_chip)), c)[1], 0)

    def each_far(act):
        lax.fori_loop(1, n_out, lambda k, c: (act(k, lax.rem(me_out + k, n_out)), c)[1], 0)

    def greet(*place):
        pl.semaphore_signal(barrier, inc=1, device_id=place, device_id_type=MESH)

    each_near(lambda k, i: greet(me_out, i))
    each_far(lambda k, o: greet(o, me_in))

    def near_copy(phase, k, source, target, i):
        return pltpu.make_async_remote_copy(
            src_ref=source, dst_ref=target, send_sem=send_sem.at[phase, k], recv_sem=recv_sem.at[phase, k],
            device_id=(me_out, i), device_id_type=MESH,
        )

    def far_copy(phase, k, source, target, o):
        return pltpu.make_async_remote_copy(
            src_ref=source, dst_ref=target, send_sem=send_sem.at[phase, k], recv_sem=recv_sem.at[phase, k],
            device_id=(o, me_in), device_id_type=MESH,
        )

    own_rows = w_ref.shape[0]
    tile = w_near.shape[1]
    per_tile = tile // own_rows
    own_w = jnp.concatenate([w_ref[...].astype(F32)] * per_tile, axis=0)
    own_w = jnp.where(iota(own_w.shape, 0) // own_rows == lax.rem(me_in, per_tile), own_w, 0.0)
    w_near[me_in] = own_w

    pl.semaphore_wait(barrier, n_in + n_out - 2)
    each_near(lambda k, i: near_copy(W_NEAR, k, w_near.at[me_in], w_near.at[me_in], i).start())

    loads[0].wait()
    loads[1].wait()
    upto = (iota((rows, rows), 0) <= iota((rows, rows), 1)).astype(F32)
    running_t = lax.dot_general(decay_ref[...], upto, NN, precision=HIGH, preferred_element_type=F32)
    dt_t = dt_ref[...]
    total_t = jnp.broadcast_to(running_t[:, rows - 1:], running_t.shape)
    columns = jnp.transpose(jnp.concatenate(
        [dt_t * jnp.exp(total_t - running_t), jnp.exp(running_t), total_t, running_t - jnp.log(dt_t)], axis=0
    ))
    shifted = columns[:, 3 * heads:]
    stack = jnp.concatenate(
        [columns[:, :heads], columns[:, heads:2 * heads], columns[:8, 2 * heads:3 * heads]], axis=0
    )
    high = stack.astype(BF16)
    rest = stack - high.astype(F32)
    middle = rest.astype(BF16)
    low = (rest - middle.astype(F32)).astype(BF16)
    stack = jnp.concatenate([high, middle, low], axis=1)
    for load in loads[2:]:
        load.wait()
    for c in range(lanes // 256):
        at = slice(c * 256, (c + 1) * 256)
        chosen = lax.rem(iota((3 * heads, 256), 0), heads) == (iota((3 * heads, 256), 1) + c * 256) // size
        wide = dot(stack, jnp.where(chosen, 1.0, 0.0).astype(BF16))
        spread[:, at] = wide[:rows]
        xw_hi[:, at], xw_lo[:, at] = split(x[:, at].astype(F32) * wide[:rows])
        gw_hi[:, at], gw_lo[:, at] = split(gy[:, at].astype(F32) * wide[rows:2 * rows])
        for q in range(max(1, 256 // part)):
            lane = c * 256 + q * part
            cut = min(part, 256)
            i = lane // part
            c_send[i % 2, i // 2, :8, lane % part:lane % part + cut] = wide[2 * rows:, q * part:q * part + cut]

    each_near(lambda k, i: near_copy(W_NEAR, k, w_near.at[me_in], w_near.at[lax.rem(me_in + n_in - k, n_in)], i).wait_recv())
    block = [
        functools.reduce(lambda a, b: a + b, [w_near[t * per_tile + q] for q in range(per_tile)])
        for t in range(n_in // per_tile)
    ]
    w_far[me_out] = jnp.concatenate(block, axis=0).astype(BF16)
    each_far(lambda k, o: far_copy(W_FAR, k, w_far.at[me_out], w_far.at[me_out], o).start())

    left = iota((rows, 2 * size), 1) < size
    keep = iota((rows, rows), 0) <= iota((rows, rows), 1)
    form = jnp.zeros((rows, rows), F32)

    def stacked(p):
        g = gy[:, p * 2 * size:(p + 1) * 2 * size]
        zero = jnp.zeros_like(g)
        return jnp.concatenate([jnp.where(left, g, zero), jnp.where(left, zero, g)], axis=0)

    for p in range(pairs):
        products = dot(x[:, p * 2 * size:(p + 1) * 2 * size], stacked(p), NT)
        for q in range(2):
            h = 2 * p + q
            spans = running_t[h:h + 1, :] - shifted[:, h:h + 1]
            factor = jnp.exp(jnp.where(keep, spans, -1e30))
            grow[h] = factor
            form = form + factor * products[:, q * rows:(q + 1) * rows]
    cut = width // n_out
    packed = cut // 2
    taken = min(packed, 128)
    for c in range(width // 128):
        turned = jnp.transpose(hidden[:, c * 128:(c + 1) * 128])
        for r in range(0, 128, taken):
            group, inside = divmod(c * 128 + r, cut)
            to = group * packed + inside % packed
            hidden_t[to:to + taken, inside // packed * rows:(inside // packed + 1) * rows] = turned[r:r + taken]

    each_far(lambda k, o: far_copy(W_FAR, k, w_far.at[me_out], w_far.at[lax.rem(me_out + n_out - k, n_out)], o).wait_recv())
    w = w_far[...].reshape(width, 2 * state)
    projected = dot(hidden[...], w)
    projected_t = jnp.transpose(projected)
    proj_hi, proj_lo = split(projected_t)
    b_t = jnp.concatenate([proj_hi[:state], proj_lo[:state]], axis=0)
    c_t = jnp.concatenate([proj_hi[state:], proj_lo[state:]], axis=0)

    def rows_of(way):
        return slice(8 + state, 8 + 2 * state) if way else slice(0, 8 + state)

    def state_rows(way, first=8):
        return slice(first + way * state, first + (way + 1) * state)

    def lanes_of(side, t):
        return pl.ds(pl.multiple_of((t * 2 + side) * part, part), part)

    def side_lanes(ref, side):
        return jnp.concatenate([ref[:, lanes_of(side, t)] for t in range(n_chip)], axis=1)

    def own_half(way, side):
        which = c_t if way else b_t
        values, rests = (gw_hi, gw_lo) if way else (xw_hi, xw_lo)
        both = dot(which, side_lanes(values, side))
        made = both[:state] + both[state:] + dot(which[:state], side_lanes(rests, side))
        for t in range(n_chip):
            c_send[side, t, state_rows(way), :] = made[:, t * part:(t + 1) * part]

    def core_out(way, k, t):
        return near_copy(C_OUT + way, k, c_send.at[other, t, rows_of(way)], c_recv.at[t, rows_of(way)], chip * 2 + other)

    def chip_out(way, k, t, source):
        return near_copy(S_OUT + way, k, s_send.at[t, rows_of(way)], s_recv.at[source, rows_of(way)], t * 2 + core)

    def each_slice(act):
        lax.fori_loop(1, n_chip + 1, lambda k, c: (act(k, lax.rem(chip + k, n_chip)), c)[1], 0)

    def give(way):
        own_half(way, other)
        each_slice(lambda k, t: core_out(way, k, t).start())

    first_core = core == 0

    def join(way):
        def one(k, t):
            core_out(way, k, t).wait_recv()
            own_total, other_total = c_send[core, t, :1, :], c_recv[t, :1, :]
            ones = jnp.ones_like(own_total)
            own_factor, other_factor = jnp.exp(other_total), jnp.exp(own_total)
            own_is_far = first_core if way == 0 else jnp.logical_not(first_core)
            at = state_rows(way)
            s_send[t, at, :] = (
                jnp.where(own_is_far, own_factor, ones) * c_send[core, t, at, :]
                + jnp.where(own_is_far, ones, other_factor) * c_recv[t, at, :]
            )
            if way == 0:
                s_send[t, :8, :] = c_send[core, t, :8, :] + c_recv[t, :8, :]

            @pl.when(k < n_chip)
            def _():
                chip_out(way, k, t, chip).start()

            @pl.when(k == n_chip)
            def _():
                s_recv[t, rows_of(way)] = s_send[t, rows_of(way)]

        each_slice(one)

    give(0)
    own_half(0, core)
    join(0)
    give(1)
    own_half(1, core)
    join(1)

    b_rows, c_rows = projected[:, :state], projected[:, state:]
    scores = dot3(b_rows, c_rows, NT)
    for p in range(pairs):
        mixed = jnp.concatenate([grow[2 * p] * scores, grow[2 * p + 1] * scores], axis=1).astype(BF16)
        gx[:, p * 2 * size:(p + 1) * 2 * size] = dot(mixed, stacked(p))
    near_b = dot3(form, c_rows)
    near_c = dot3(jnp.transpose(form), b_rows)

    servers = n_out // 2

    def far_send(q, k, o):
        @pl.when(o // servers == q)
        def _():
            far_copy(S_FAR, k, o_send.at[o], o_recv.at[me_out], o).start()

    def far_step(forward):
        o_recv[me_out] = o_send[me_out]
        each_far(lambda k, o: far_copy(S_FAR, k, o_send.at[o], o_recv.at[lax.rem(me_out + n_out - k, n_out)], o).wait_recv())
        held = jnp.zeros((far, part), F32)
        for k in range(n_out):
            at = k if forward else n_out - 1 - k
            o_back[at] = held
            held = held * jnp.exp(o_recv[at, far:far + 1, :]) + o_recv[at, :far, :]
        each_far(lambda k, o: far_copy(S_BACK, k, o_back.at[o], carry.at[me_out], o).start())
        carry[me_out] = o_back[me_out]

    for way in range(WAYS):
        each_chip(lambda k, t: chip_out(way, k, t, lax.rem(chip + n_chip - k, n_chip)).wait_recv())
        if way == 0:
            totals = [s_recv[k, :1, :] for k in range(n_chip)]
            after, before = jnp.zeros((1, part), F32), jnp.zeros((1, part), F32)
            ahead, behind = [None] * n_chip, [None] * n_chip
            for k in range(n_chip):
                ahead[k], behind[n_chip - 1 - k] = jnp.exp(before), jnp.exp(after)
                before = before + totals[k]
                after = after + totals[n_chip - 1 - k]
            steps = [jnp.exp(t) for t in totals]
        held = jnp.zeros((state, part), F32)
        for k in range(n_chip - 1, -1, -1) if way else range(n_chip):
            prefix[k, state_rows(way, 0), :] = held
            held = held * steps[k] + s_recv[k, state_rows(way), :]
        for j in range(servers):
            o_send[way * servers + j, :far, :] = held[j * far:(j + 1) * far]
            o_send[way * servers + j, far:, :] = jnp.broadcast_to(before, (8, part))
        each_far(functools.partial(far_send, way))
    for forward in (True, False):
        pl.when((me_out < n_out // 2) == forward)(functools.partial(far_step, forward))

    def back_wait(q, k, o):
        source = lax.rem(me_out + n_out - k, n_out)

        @pl.when(source // servers == q)
        def _():
            far_copy(S_BACK, k, o_back.at[o], carry.at[source], o).wait_recv()

    def home_copy(way, k, t, source):
        at = state_rows(way, 0)
        return near_copy(S_HOME + way, k, s_back.at[t, at], s_home.at[source, at], t * 2 + core)

    for way in range(WAYS):
        each_far(functools.partial(back_wait, way))
        carried = jnp.concatenate([carry[way * servers + j] for j in range(servers)], axis=0)
        reach = behind if way else ahead
        at = state_rows(way, 0)
        for k in range(n_chip):
            s_back[k, at, :] = prefix[k, at, :] + reach[k] * carried
        each_chip(lambda k, t: home_copy(way, k, t, chip).start())
        s_home[chip, at, :] = s_back[chip, at, :]

    def core_home(way, k, side, t):
        at = state_rows(way, 0)
        return near_copy(C_HOME + way, k, c_back.at[t, at], states.at[side, t, at], chip * 2 + other)

    def use_half(way, side, sum_):
        values, rests = (xw_hi, xw_lo) if way else (gw_hi, gw_lo)
        got = jnp.concatenate([states[side, t, state_rows(way, 0), :] for t in range(n_chip)], axis=1)
        got_hi, got_lo = split(got)
        both = dot(side_lanes(values, side), jnp.concatenate([got_hi, got_lo], axis=0), NT)
        return sum_ + both[:, :state] + both[:, state:] + dot(side_lanes(rests, side), got_hi, NT)

    def source_of(k):
        return lax.rem(chip + n_chip - k, n_chip)

    def share(way, k):
        t = source_of(k)
        at, tall = state_rows(way, 0), state_rows(way)
        got = s_home[t, at, :]
        by_own = jnp.exp(c_send[core, t, :1, :]) * got + c_send[core, t, tall, :]
        by_other = jnp.exp(c_recv[t, :1, :]) * got + c_recv[t, tall, :]
        comes_first = first_core if way == 0 else jnp.logical_not(first_core)
        states[core, t, at, :] = jnp.where(comes_first, got, by_other)
        c_back[t, at, :] = jnp.where(comes_first, by_own, got)
        core_home(way, k, core, t).start()

    def term_copy(way, k, o, source):
        return far_copy(G_FAR + way, k, g_send.at[way, o], g_recv.at[way, source], o)

    def send_term(way, low):
        zero = jnp.zeros_like(low)
        pair = jnp.concatenate(
            [jnp.concatenate([low, zero], axis=1), jnp.concatenate([zero, low], axis=1)], axis=0
        )
        term = (dot(hidden_t[...], pair) * scale).astype(BF16)
        for o in range(n_out):
            g_send[way, o] = term[o * packed:(o + 1) * packed]
        each_far(lambda k, o: term_copy(way, k, o, me_out).start())
        g_recv[way, me_out] = g_send[way, me_out]

    sums = []
    for way, near in enumerate((near_c, near_b)):
        def share_arrived(k, t):
            source = source_of(k)
            home_copy(way, k, source, source).wait_recv()
            share(way, k)

        share(way, 0)
        each_chip(share_arrived)
        sum_ = use_half(way, core, near)
        each_slice(lambda k, t: core_home(way, k - 1, other, source_of(k - 1)).wait_recv())
        sums.append(use_half(way, other, sum_).astype(BF16))
        send_term(way, sums[way])
    d_low = jnp.concatenate(sums[::-1], axis=1)

    gh[...] = dot(d_low, w, NT)
    store_gh = pltpu.make_async_copy(gh, gh_hbm, load_sem.at[0])
    store_gh.start()

    b_hi, b_lo = split(b_rows)
    b_three = jnp.concatenate([b_hi, b_lo, b_hi], axis=1)
    for i in range(n_in):
        at = slice(i * part, (i + 1) * part)
        got_hi, got_lo = split(states[i % 2, i // 2, state:, :])
        gx[:, at] = gx[:, at] + spread[:, at] * dot(b_three, jnp.concatenate([got_hi, got_hi, got_lo], axis=0))
    store_gx = pltpu.make_async_copy(gx, gx_hbm, load_sem.at[1])
    store_gx.start()

    halves = []
    for way in range(WAYS):
        each_far(lambda k, o: term_copy(way, k, o, lax.rem(me_out + n_out - k, n_out)).wait_recv())
        halves.append(functools.reduce(lambda a, b: a + b, [g_recv[way, o].astype(F32) for o in range(n_out)]))
    g_sum[:packed] = jnp.concatenate([halves[1][:, :state], halves[0][:, :state]], axis=1)
    g_sum[packed:] = jnp.concatenate([halves[1][:, state:], halves[0][:, state:]], axis=1)

    def owned(i):
        return g_sum.at[pl.ds(pl.multiple_of(i // per_tile * tile, tile), tile), :]

    each_near(lambda k, i: near_copy(G_NEAR, k, owned(i), g_near.at[me_in], i).start())
    g_near[me_in] = g_sum[pl.ds(pl.multiple_of(me_in // per_tile * tile, tile), tile), :]

    each_near(lambda k, i: near_copy(W_NEAR, k, w_near.at[me_in], w_near.at[me_in], i).wait_send())
    each_far(lambda k, o: far_copy(W_FAR, k, w_far.at[me_out], w_far.at[me_out], o).wait_send())
    for way in range(WAYS):
        each_slice(lambda k, t: core_out(way, k, t).wait_send())
        each_chip(lambda k, t: chip_out(way, k, t, chip).wait_send())
        each_chip(lambda k, t: home_copy(way, k, t, chip).wait_send())
        each_slice(lambda k, t: core_home(way, k - 1, core, source_of(k - 1)).wait_send())
    each_far(lambda k, o: far_copy(S_FAR, k, o_send.at[o], o_recv.at[me_out], o).wait_send())
    each_far(lambda k, o: far_copy(S_BACK, k, o_back.at[o], carry.at[me_out], o).wait_send())
    for way in range(WAYS):
        each_far(lambda k, o: term_copy(way, k, o, me_out).wait_send())
    each_near(lambda k, i: near_copy(G_NEAR, k, owned(i), g_near.at[lax.rem(me_in + n_in - k, n_in)], i).wait_recv())
    summed = functools.reduce(lambda a, b: a + b, [g_near[i] for i in range(n_in)])
    mine = summed[:own_rows]
    for q in range(1, per_tile):
        mine = jnp.where(lax.rem(me_in, per_tile) == q, summed[q * own_rows:(q + 1) * own_rows], mine)
    gp_ref[...] = mine

    each_near(lambda k, i: near_copy(G_NEAR, k, owned(i), g_near.at[me_in], i).wait_send())
    store_gh.wait()
    store_gx.wait()


def write_out(gx_from, gh_from, gp_from, gx_to, gh_to, gp_to, gx, gh, gp, sem):
    pieces = gx.shape[1]
    moves = [(gp_from, gp, gp_to)]
    for q in range(gx.shape[0]):
        at = slice(q * pieces, (q + 1) * pieces)
        moves.append((gx_from.at[at], gx.at[q], gx_to.at[at]))
        moves.append((gh_from.at[at], gh.at[q], gh_to.at[at]))
    reads = [pltpu.make_async_copy(m[0], m[1], sem.at[0, k]) for k, m in enumerate(moves)]
    writes = [pltpu.make_async_copy(m[1], m[2], sem.at[1, k]) for k, m in enumerate(moves)]
    for read in reads:
        read.start()
    for read, write in zip(reads, writes):
        read.wait()
        write.start()
    for write in writes:
        write.wait()


def per_device(hidden, x_act, dt_step, log_decay, w_bc, grad_y):
    n_out, n_in = lax.axis_size("outer"), lax.axis_size("inner")
    rows, width = hidden.shape
    lanes = x_act.shape[1]
    heads = dt_step.shape[1]
    own_rows, columns = w_bc.shape
    part = lanes // n_in
    far = columns // n_out
    tile = max(8, own_rows)
    most = max(n_out, n_in)
    scale = 1.0 / math.sqrt(rows * n_out * n_in)
    anywhere = pl.BlockSpec(memory_space=pl.ANY)
    vmem = pl.BlockSpec(memory_space=pltpu.VMEM)
    results = pl.pallas_call(
        functools.partial(kernel, scale, n_out, n_in),
        out_shape=(
            jax.ShapeDtypeStruct((rows, lanes), F32),
            jax.ShapeDtypeStruct((rows, width), F32),
            jax.ShapeDtypeStruct((own_rows, columns), F32),
        ),
        in_specs=[anywhere, anywhere, anywhere, anywhere, vmem, anywhere],
        out_specs=(anywhere, anywhere, vmem),
        scratch_shapes=[
            pltpu.VMEM((rows, width), BF16),
            pltpu.VMEM((rows, lanes), BF16),
            pltpu.VMEM((rows, lanes), BF16),
            pltpu.VMEM((heads, rows), F32),
            pltpu.VMEM((heads, rows), F32),
            pltpu.VMEM((width // 2, 2 * rows), BF16),
            pltpu.VMEM((rows, lanes), F32),
            pltpu.VMEM((rows, width), F32),
            pltpu.VMEM((n_in, tile, columns), F32),
            pltpu.VMEM((n_out, width // n_out, columns), BF16),
            pltpu.VMEM((heads, rows, rows), F32),
            pltpu.VMEM((rows, lanes), F32),
            pltpu.VMEM((rows, lanes), BF16),
            pltpu.VMEM((rows, lanes), BF16),
            pltpu.VMEM((rows, lanes), BF16),
            pltpu.VMEM((rows, lanes), BF16),
            pltpu.VMEM((2, n_in // 2, columns + 8, part), F32),
            pltpu.VMEM((n_in // 2, columns + 8, part), F32),
            pltpu.VMEM((n_in // 2, columns + 8, part), F32),
            pltpu.VMEM((n_in // 2, columns + 8, part), F32),
            pltpu.VMEM((n_in // 2, columns, part), F32),
            pltpu.VMEM((n_out, far + 8, part), F32),
            pltpu.VMEM((n_out, far + 8, part), F32),
            pltpu.VMEM((n_out, far, part), F32),
            pltpu.VMEM((n_out, far, part), F32),
            pltpu.VMEM((n_in // 2, columns, part), F32),
            pltpu.VMEM((n_in // 2, columns, part), F32),
            pltpu.VMEM((n_in // 2, columns, part), F32),
            pltpu.VMEM((2, n_in // 2, columns, part), F32),
            pltpu.VMEM((2, n_out, width // n_out // 2, columns), BF16),
            pltpu.VMEM((2, n_out, width // n_out // 2, columns), BF16),
            pltpu.VMEM((width // n_out, columns), F32),
            pltpu.VMEM((n_in, tile, columns), F32),
            pltpu.SemaphoreType.DMA((5,)),
            pltpu.SemaphoreType.DMA((PHASES, most)),
            pltpu.SemaphoreType.DMA((PHASES, most)),
        ],
        compiler_params=pltpu.CompilerParams(
            collective_id=0, has_side_effects=True, vmem_limit_bytes=60 * 1024 * 1024
        ),
        cost_estimate=pl.CostEstimate(flops=10**9, bytes_accessed=3 * 10**6, transcendentals=10**6),
    )(hidden, x_act, dt_step.T, log_decay.T, w_bc, grad_y)
    pieces = rows // 4
    return pl.pallas_call(
        write_out,
        out_shape=tuple(jax.ShapeDtypeStruct(r.shape, r.dtype) for r in results),
        in_specs=[anywhere] * 3,
        out_specs=(anywhere,) * 3,
        scratch_shapes=[
            pltpu.VMEM((4, pieces, lanes), F32),
            pltpu.VMEM((4, pieces, width), F32),
            pltpu.VMEM((own_rows, columns), F32),
            pltpu.SemaphoreType.DMA((2, 9)),
        ],
        compiler_params=pltpu.CompilerParams(vmem_limit_bytes=60 * 1024 * 1024),
    )(*results)


def solution(mesh):
    spec = P(("outer", "inner"), None)
    return jax.shard_map(
        per_device, mesh=mesh, in_specs=(spec,) * 6, out_specs=(spec,) * 3, check_vma=False
    )
```
